256 devices in a mesh: blk: 8 (over y, x_hi), dom: 32 (over z, x_lo, core).
Axes of the slice: x: 4 (x_hi: 2, x_lo: 2; x = x_hi * 2 + x_lo), y: 4, z: 8, core: 2. Of those that a mesh axis runs over, the one named last changes fastest.
Arguments:
- cell_features: bfloat16 [32, 2048, 768], P('dom', 'blk'), may hold values from -6 to 6
- cotangent: bfloat16 [32, 2048, 768], P('dom', 'blk'), may hold values from -6 to 6
- query_weight: bfloat16 [768, 768], replicated
- key_weight: bfloat16 [768, 768], replicated
- value_weight: bfloat16 [768, 768], replicated, may hold values from -0.21875 to 0.21875
- out_weight: bfloat16 [768, 768], replicated, may hold values from -0.21875 to 0.21875
- anchor_index: int32 [32, 256], P('dom', 'blk'), may hold values from 0 to 255, as said below
- face_cells: int32 [32, 8, 2, 128], P('dom', 'blk'), may hold values from 0 to 255, as said below
- halo_count: int32 [32, 8, 2], P('dom', 'blk'), may hold values from 0 to 128, as said below
- neighbour_blocks: int32 [32, 16, 3], P('dom', 'blk'), may hold values from 0 to 3, as said below
Outputs:
- mixed: bfloat16 [32, 2048, 768], P('dom', 'blk')
- cell_grad: bfloat16 [32, 2048, 768], P('dom', 'blk')
- weight_grads: float32 [3072, 768], P(('blk', 'dom'))
The draws below stay inside these ranges and needn't reach their ends.
Inputs may be any that keep to these rules, and one draw needn't show every extreme that they name: `anchor_index`: the 32 entries of one slot are different cells of that slot. `face_cells`: the 256 entries of one slot are different cells of that slot. halo_count[0, b, 0] and halo_count[31, b, 1] are 0 for every b; all other entries are 1 or more. `neighbour_blocks`: row b*2+j lists 3 different pool blocks, the first of them j itself.
All inputs are finite; a program needn't handle non-finite values.
Results may differ from the reference program's by a relative error of at most 0.017.
The reference program's roundings to bfloat16 on the way count: a program that leaves them out, or rounds other values in their place, can miss the bound.
Values may be sent and summed in bfloat16 or wider, within the bound.
No kernel may reach another device: no remote copies, remote signals or barrier semaphores. Data moves between devices by JAX's collectives and lax.ppermute only.
A program may use at most 128 MiB of HBM per device.

```python
import math
import jax
import jax.numpy as jnp
from jax import lax

D = 768
HEADS = 12
BS = 128
NB = 3
C_DEV = 256
A_DEV = 32
QBLOCKS = 2
POOL = 4
PARTS_SIZE = 32
PART_CELLS = 2048
N_BLK = 8


def own_matrix(key):
    return jax.random.normal(key, (D, D), jnp.float32) / math.sqrt(D)


def draw_query_weight(key, part):
    key = jax.random.fold_in(key, 1)
    own = own_matrix(key)
    return own.astype(jnp.bfloat16)


def draw_key_weight(key, part):
    key = jax.random.fold_in(key, 2)
    own = own_matrix(key)
    return own.astype(jnp.bfloat16)


def slot_choice(key, amount):
    slot_keys = jax.random.split(key, PARTS_SIZE * N_BLK)

    def pick_slot(slot_key):
        return jax.random.permutation(slot_key, C_DEV)[:amount]
    return jax.vmap(pick_slot)(slot_keys).astype(jnp.int32)


def draw_anchor_index(key, part):
    key = jax.random.fold_in(key, 3)
    chosen = slot_choice(key, A_DEV)
    return chosen.reshape(PARTS_SIZE, N_BLK * A_DEV)


def draw_face_cells(key, part):
    key = jax.random.fold_in(key, 4)
    chosen = slot_choice(key, 2 * BS)
    return chosen.reshape(PARTS_SIZE, N_BLK, 2, BS)


def draw_halo_count(key, part):
    key = jax.random.fold_in(key, 5)
    drawn = jax.random.randint(key, (PARTS_SIZE, N_BLK, 2), 1, BS + 1)
    part_index = jnp.arange(PARTS_SIZE)[:, None, None]
    side = jnp.arange(2)[None, None, :]
    edge = (part_index == 0) & (side == 0) | (part_index == PARTS_SIZE - 1) & (side == 1)
    drawn = jnp.where(edge, 0, drawn)
    where_full = jax.random.randint(jax.random.fold_in(key, 9), (2,), 0, 1 << 20)
    full_part = 1 + where_full[0] % (PARTS_SIZE - 1)
    full_slot = where_full[1] % N_BLK
    drawn = drawn.at[full_part, full_slot, 0].set(BS)
    return drawn.astype(jnp.int32)


def draw_neighbour_blocks(key, part):
    key = jax.random.fold_in(key, 6)
    row_total = PARTS_SIZE * N_BLK * QBLOCKS
    raw = jax.random.randint(key, (row_total, POOL - 1), 0, 1 << 20)
    ranking = raw * POOL + jnp.arange(POOL - 1)[None, :]
    unused, picked = lax.top_k(ranking, NB - 1)
    itself = jnp.arange(row_total) % QBLOCKS
    others = (itself[:, None] + 1 + picked) % POOL
    table = jnp.concatenate([itself[:, None], others], 1).astype(jnp.int32)
    return table.reshape(PARTS_SIZE, N_BLK * QBLOCKS, NB)


def block_scale(stream_key, shape, pieces, least, largest):
    def one(dim, shards_of):
        heights = jax.random.uniform(jax.random.fold_in(jax.random.fold_in(stream_key, 6), dim), (shards_of,), jnp.float32, least / len(pieces), largest / len(pieces))
        return jnp.repeat(jnp.exp(heights), shape[dim] // shards_of).reshape((-1,) + (1,) * (len(shape) - dim - 1))

    factor_of = one(*pieces[0])
    for cut in pieces[1:]:
        factor_of = factor_of * one(*cut)
    return factor_of


def centred(rng, extent, deviation, most, cuts=(), kind=jnp.bfloat16):
    values = jax.random.normal(rng, extent, jnp.float32) * deviation
    if len(cuts) > 0:
        values = block_scale(rng, extent, cuts, -0.22, 0.18) * values
    return jnp.clip(values, min=-most, max=most).astype(kind)


def setup_inputs(seed: int = 0) -> dict:
    keys = jax.random.split(jax.random.key(seed), 11)
    cell_features = centred(keys[0], (PARTS_SIZE, PART_CELLS, D), 1.0, 6.0, ((0, 32), (1, 8)))
    cotangent = centred(keys[1], (PARTS_SIZE, PART_CELLS, D), 1.0, 6.0, ((0, 32), (1, 8)))
    query_weight = draw_query_weight(jax.random.fold_in(keys[10], 71), 0)
    key_weight = draw_key_weight(jax.random.fold_in(keys[10], 71), 0)
    value_weight = centred(keys[4], (D, D), D ** -0.5, 0.21875)
    out_weight = centred(keys[5], (D, D), D ** -0.5, 0.21875)
    anchor_index = draw_anchor_index(jax.random.fold_in(keys[10], 71), 0)
    face_cells = draw_face_cells(jax.random.fold_in(keys[10], 71), 0)
    halo_count = draw_halo_count(jax.random.fold_in(keys[10], 71), 0)
    neighbour_blocks = draw_neighbour_blocks(jax.random.fold_in(keys[10], 71), 0)
    return dict(cell_features=cell_features, cotangent=cotangent, query_weight=query_weight, key_weight=key_weight, value_weight=value_weight, out_weight=out_weight, anchor_index=anchor_index, face_cells=face_cells, halo_count=halo_count, neighbour_blocks=neighbour_blocks)


EPSILON = 1e-06
MASKED = -1e+30

def rounded(tensor):
    return lax.optimization_barrier(tensor.astype(jnp.bfloat16)).astype(jnp.float32)

def split_heads(tensor):
    leading = tensor.shape[:-2]
    length = tensor.shape[-2]
    tensor = tensor.reshape(leading + (length, HEADS, tensor.shape[-1] // HEADS))
    return jnp.moveaxis(tensor, -2, -3)

def join_heads(tensor):
    tensor = jnp.moveaxis(tensor, -3, -2)
    return tensor.reshape(tensor.shape[:-2] + (tensor.shape[-2] * tensor.shape[-1],))

def attend(queries, key_rows, value_rows, upstream, validity):
    scaling = 1.0 / math.sqrt(queries.shape[-1])
    q_float = queries.astype(jnp.float32)
    k_float = key_rows.astype(jnp.float32)
    v_float = value_rows.astype(jnp.float32)
    g_float = upstream.astype(jnp.float32)
    scores = jnp.einsum('...qe,...ke->...qk', q_float, k_float) * scaling
    scores = jnp.where(validity[..., None, :], scores, MASKED)
    highest = lax.optimization_barrier(jnp.max(scores, axis=-1, keepdims=True))
    powers = jnp.exp(scores - highest)
    probability = powers / lax.optimization_barrier(jnp.sum(powers, axis=-1, keepdims=True))
    prob_rounded = rounded(probability)
    out_rows = jnp.einsum('...qk,...ke->...qe', prob_rounded, v_float)
    prob_grad = jnp.einsum('...qe,...ke->...qk', g_float, v_float)
    score_grad = probability * (prob_grad - lax.optimization_barrier(jnp.sum(probability * prob_grad, axis=-1, keepdims=True)))
    score_rounded = rounded(score_grad)
    query_term = jnp.einsum('...qk,...ke->...qe', score_rounded, k_float) * scaling
    key_term = jnp.einsum('...qk,...qe->...ke', score_rounded, q_float) * scaling
    value_term = jnp.einsum('...qk,...qe->...ke', prob_rounded, g_float)
    return (out_rows, query_term, key_term, value_term)

def take_rows(table, index):
    return table[index]

def scatter_rows(base, index, addend):
    return base.at[index].add(addend)

def reference(cell_features, cotangent, query_weight, key_weight, value_weight, out_weight, anchor_index, face_cells, halo_count, neighbour_blocks):
    slot_count = PARTS_SIZE * N_BLK
    block_count = C_DEV // BS
    row_total = slot_count * C_DEV
    pick_rows = jax.vmap(take_rows)
    x_slot = cell_features.reshape(slot_count, C_DEV, D)
    dy_slot = cotangent.reshape(slot_count, C_DEV, D)
    as_float = x_slot.astype(jnp.float32)
    inverse = lax.rsqrt(lax.optimization_barrier(jnp.mean(as_float * as_float, axis=-1, keepdims=True)) + EPSILON)
    normed = (as_float * inverse).astype(jnp.bfloat16)
    flat = normed.reshape(row_total, D)

    def project(weight):
        return jnp.dot(flat, weight, preferred_element_type=jnp.float32).astype(jnp.bfloat16).reshape(slot_count, C_DEV, D)
    queries = project(query_weight)
    key_cells = project(key_weight)
    value_cells = project(value_weight)
    grad_mid = jnp.dot(dy_slot.reshape(row_total, D), out_weight.T, preferred_element_type=jnp.float32)
    grad_mid = grad_mid.astype(jnp.bfloat16).reshape(slot_count, C_DEV, D)
    anchor_rows = anchor_index.reshape(slot_count, A_DEV)
    anchor_keys = pick_rows(key_cells, anchor_rows).reshape(PARTS_SIZE, N_BLK * A_DEV, D)
    anchor_values = pick_rows(value_cells, anchor_rows).reshape(PARTS_SIZE, N_BLK * A_DEV, D)
    face_rows = face_cells.reshape(slot_count, 2 * BS)
    sent_keys = pick_rows(key_cells, face_rows).reshape(PARTS_SIZE, N_BLK, 2, BS, D)
    sent_values = pick_rows(value_cells, face_rows).reshape(PARTS_SIZE, N_BLK, 2, BS, D)
    zeros_block = jnp.zeros((1, N_BLK, BS, D), jnp.bfloat16)

    def pool_of(local, sent):
        lower = jnp.concatenate([zeros_block, sent[:-1, :, 1]], 0).reshape(slot_count, 1, BS, D)
        upper = jnp.concatenate([sent[1:, :, 0], zeros_block], 0).reshape(slot_count, 1, BS, D)
        return jnp.concatenate([local.reshape(slot_count, block_count, BS, D), lower, upper], 1)
    key_pool = pool_of(key_cells, sent_keys)
    value_pool = pool_of(value_cells, sent_values)
    live_count = halo_count.reshape(slot_count, 2)
    positions = jnp.arange(BS)
    live_rows = jnp.concatenate([jnp.ones((slot_count, block_count, BS), bool), (positions[None, :] < live_count[:, 0:1])[:, None], (positions[None, :] < live_count[:, 1:2])[:, None]], 1)
    near_index = neighbour_blocks.reshape(slot_count, block_count, NB)
    chosen_keys = pick_rows(key_pool, near_index)
    chosen_values = pick_rows(value_pool, near_index)
    chosen_live = pick_rows(live_rows, near_index)

    def by_part(tensor):
        return tensor.reshape((PARTS_SIZE, N_BLK) + tensor.shape[1:])

    def partition(members):
        q_part, g_part, keys_part, values_part, live_part, near_part, akey_part, aval_part = members
        akey_heads = split_heads(akey_part)
        aval_heads = split_heads(aval_part)
        all_live = jnp.ones((N_BLK * A_DEV,), bool)

        def slot_pass(totals, slot):
            q_slot, g_slot, keys_slot, values_slot, live_slot, near_slot = slot
            anchor_out, anchor_dquery, anchor_dkey, anchor_dvalue = attend(split_heads(q_slot), akey_heads, aval_heads, split_heads(g_slot), all_live)
            near_out, near_dquery, near_dkey, near_dvalue = attend(split_heads(q_slot.reshape(block_count, BS, D)), split_heads(keys_slot.reshape(block_count, NB * BS, D)), split_heads(values_slot.reshape(block_count, NB * BS, D)), split_heads(g_slot.reshape(block_count, BS, D)), live_slot.reshape(block_count, 1, NB * BS))
            attended = (join_heads(anchor_out) + join_heads(near_out).reshape(C_DEV, D)).astype(jnp.bfloat16)
            query_sum = join_heads(anchor_dquery) + join_heads(near_dquery).reshape(C_DEV, D)
            chosen_grad = jnp.concatenate([join_heads(near_dkey), join_heads(near_dvalue)], -1)
            chosen_grad = chosen_grad.reshape(block_count * NB, BS, 2 * D)
            pool_grad = jnp.zeros((block_count + 2, BS, 2 * D), jnp.float32).at[near_slot.reshape(-1)].add(chosen_grad)
            anchor_term = jnp.concatenate([join_heads(anchor_dkey), join_heads(anchor_dvalue)], -1)
            return (totals + rounded(anchor_term), (attended, query_sum, pool_grad))
        start = jnp.zeros((N_BLK * A_DEV, 2 * D), jnp.float32)
        anchor_grad, outputs = lax.scan(slot_pass, start, (q_part, g_part, keys_part, values_part, live_part, near_part))
        return outputs + (anchor_grad,)
    attended, query_sum, pool_grad, anchor_grad = lax.map(partition, (by_part(queries), by_part(grad_mid), by_part(chosen_keys), by_part(chosen_values), by_part(chosen_live), by_part(near_index), anchor_keys, anchor_values))
    attended = attended.reshape(slot_count, C_DEV, D)
    query_sum = query_sum.reshape(slot_count, C_DEV, D)
    pool_grad = pool_grad.reshape(slot_count, block_count + 2, BS, 2 * D)
    anchor_share = anchor_grad.reshape(slot_count, A_DEV, 2 * D)
    halo_grad = rounded(pool_grad[:, block_count:]).reshape(PARTS_SIZE, N_BLK, 2, BS, 2 * D)
    zeros_grad = jnp.zeros((1, N_BLK, BS, 2 * D), jnp.float32)
    to_lower = jnp.concatenate([zeros_grad, halo_grad[:-1, :, 1]], 0)
    to_upper = jnp.concatenate([halo_grad[1:, :, 0], zeros_grad], 0)
    came_back = jnp.stack([to_lower, to_upper], 2).reshape(slot_count, 2 * BS, 2 * D)
    keyval_grad = pool_grad[:, :block_count].reshape(slot_count, C_DEV, 2 * D)
    keyval_grad = jax.vmap(scatter_rows)(keyval_grad, anchor_rows, anchor_share)
    keyval_grad = jax.vmap(scatter_rows)(keyval_grad, face_rows, came_back)
    query_grad = query_sum.astype(jnp.bfloat16)
    key_grad = keyval_grad[..., :D].astype(jnp.bfloat16)
    value_grad = keyval_grad[..., D:].astype(jnp.bfloat16)

    def outer_sum(left, right):
        return jnp.dot(left.reshape(row_total, D).T, right.reshape(row_total, D), preferred_element_type=jnp.float32)
    weight_grads = jnp.concatenate([outer_sum(normed, query_grad), outer_sum(normed, key_grad), outer_sum(normed, value_grad), outer_sum(attended, dy_slot)], 0)

    def back_project(grad_rows, weight):
        return jnp.dot(grad_rows.reshape(row_total, D), weight.T, preferred_element_type=jnp.float32).reshape(slot_count, C_DEV, D)
    normed_grad = back_project(query_grad, query_weight) + back_project(key_grad, key_weight) + back_project(value_grad, value_weight)
    cot_float = dy_slot.astype(jnp.float32)
    cube = inverse * inverse * inverse
    cell_grad = cot_float + inverse * normed_grad - as_float * cube * lax.optimization_barrier(jnp.mean(normed_grad * as_float, axis=-1, keepdims=True))
    mixed = as_float + jnp.dot(attended.reshape(row_total, D), out_weight, preferred_element_type=jnp.float32).reshape(slot_count, C_DEV, D)
    mixed = mixed.astype(jnp.bfloat16).reshape(PARTS_SIZE, N_BLK * C_DEV, D)
    cell_grad = cell_grad.astype(jnp.bfloat16).reshape(PARTS_SIZE, N_BLK * C_DEV, D)
    return (mixed, cell_grad, weight_grads)
```

```python
import jax
import jax.numpy as jnp
from jax import lax
from jax.experimental import pallas as pl
from jax.experimental.pallas import tpu as pltpu
from jax.sharding import Mesh, PartitionSpec as P

HEADS = 12
BS = 128
NB = 3
D = 768
CELLS = 256
ANCHORS = 256
POOL_ROWS = 512
KEY_ROWS = 768
HEAD = 64
SIDE = 384
PAIR = 128
SCALE = 0.125
EPSILON = 1e-06
MASKED = -1e30

f32 = jnp.float32
bf16 = jnp.bfloat16

NN = (((1,), (0,)), ((), ()))
NT = (((1,), (1,)), ((), ()))
TN = (((0,), (0,)), ((), ()))


def dot(a, b, dims=NN):
    return lax.dot_general(a, b, dims, preferred_element_type=f32)


def params(mib):
    return pltpu.CompilerParams(vmem_limit_bytes=mib << 20)


def send_kernel(x_ref, anchor_ref, face_ref, normed_ref, rows_a_ref, rows_lo_ref, rows_hi_ref):
    x = x_ref[...].astype(f32)
    inverse = lax.rsqrt(jnp.mean(x * x, axis=-1, keepdims=True) + EPSILON)
    normed = (x * inverse).astype(bf16)
    normed_ref[...] = normed

    def picked(index_row):
        cells = lax.broadcasted_iota(jnp.int32, (CELLS, index_row.shape[1]), 0)
        one_hot = (cells == index_row).astype(bf16)
        return dot(one_hot, normed, TN).astype(bf16)

    rows_a_ref[...] = picked(anchor_ref[...])
    rows_lo_ref[...] = picked(face_ref[0:1, :])
    rows_hi_ref[...] = picked(face_ref[1:2, :])


def send_call(x, anchor_row, face_rows):
    shapes = [(CELLS, D), (32, D), (BS, D), (BS, D)]
    return pl.pallas_call(
        send_kernel,
        out_shape=[jax.ShapeDtypeStruct(s, bf16) for s in shapes],
        compiler_params=params(32),
    )(x, anchor_row, face_rows)


def project_kernel(n_ref, dy_ref, wq_ref, wk_ref, wv_ref, wo_ref, q_ref, k_ref, v_ref, g_ref):
    normed = n_ref[...]
    q_ref[...] = (dot(normed, wq_ref[...]).astype(bf16) * SCALE).astype(bf16)
    k_ref[...] = dot(normed, wk_ref[...]).astype(bf16)
    v_ref[...] = dot(normed, wv_ref[...]).astype(bf16)
    g_ref[...] = dot(dy_ref[...], wo_ref[...], NT).astype(bf16)


def project_call(normed, dy, wq, wk, wv, wo):
    return pl.pallas_call(
        project_kernel,
        out_shape=[jax.ShapeDtypeStruct((CELLS, D), bf16)] * 4,
        compiler_params=params(32),
    )(normed, dy, wq, wk, wv, wo)


def attend_kernel(
    near_ref, count_ref, core_ref, q_ref, k_ref, v_ref, g_ref, n_ref, lo_ref, hi_ref, an_ref, dy_ref,
    wk_ref, wv_ref,
    att_ref, qg_ref, kg_ref, vg_ref, keep_ref, send_ref,
    keys, values, keys_t, values_t, bias, att_t, normed_all,
):
    normed_all[0:CELLS, :] = n_ref[...]
    normed_all[CELLS:CELLS + BS, :] = lo_ref[...]
    normed_all[CELLS + BS:POOL_ROWS, :] = hi_ref[...]
    normed_all[POOL_ROWS:, :] = an_ref[...]
    outside = normed_all[CELLS:, :]
    keys[0:CELLS, :] = k_ref[...]
    values[0:CELLS, :] = v_ref[...]
    keys[CELLS:, :] = dot(outside, wk_ref[...]).astype(bf16)
    values[CELLS:, :] = dot(outside, wv_ref[...]).astype(bf16)
    keys_t[...] = keys[...].T
    values_t[...] = values[...].T

    row = lax.broadcasted_iota(jnp.int32, (BS, BS), 0)
    for block in range(4):
        for j in range(2):
            used = (near_ref[j, 0] == block) | (near_ref[j, 1] == block) | (near_ref[j, 2] == block)
            live = jnp.where(used, BS if block < 2 else count_ref[max(block - 2, 0)], 0)
            bias[block * BS:(block + 1) * BS, j * BS:(j + 1) * BS] = jnp.where(row < live, 0.0, MASKED)

    lane = lax.broadcasted_iota(jnp.int32, (CELLS, PAIR), 1)

    def softmax(scores):
        highest = jnp.max(scores, axis=0, keepdims=True)
        powers = jnp.exp(scores - highest)
        return powers * (1.0 / jnp.sum(powers, axis=0, keepdims=True))

    def score_grad(probs, prob_grad):
        weighted = probs * prob_grad
        return weighted - probs * jnp.sum(weighted, axis=0, keepdims=True)

    def pair_step(pair, carry):
        start = pl.multiple_of(pair * PAIR, PAIR)
        cols = pl.ds(start, PAIR)
        k_pair = keys[:, cols]
        v_pair = values[:, cols]
        q_pair = q_ref[:, cols]
        g_pair = g_ref[:, cols]
        key_term = None
        value_term = None
        out_t = []
        qg_t = []
        for half in range(2):
            mine = (lane >= HEAD) if half else (lane < HEAD)
            q_head = jnp.where(mine, q_pair, jnp.zeros_like(q_pair))
            g_head = jnp.where(mine, g_pair, jnp.zeros_like(g_pair))
            scores = dot(k_pair, q_head, NT)
            prob_grad = dot(v_pair, g_head, NT)
            near = softmax(scores[:POOL_ROWS] + bias[...])
            anchor = softmax(scores[POOL_ROWS:])
            probs = jnp.concatenate([near.astype(bf16), anchor.astype(bf16)], 0)
            grads = jnp.concatenate(
                [
                    score_grad(near, prob_grad[:POOL_ROWS]).astype(bf16),
                    score_grad(anchor, prob_grad[POOL_ROWS:]).astype(bf16),
                ],
                0,
            )
            head_rows = pl.ds(pl.multiple_of(start + half * HEAD, HEAD), HEAD)
            out_t.append(dot(values_t[head_rows, :], probs))
            qg_t.append(dot(keys_t[head_rows, :], grads) * SCALE)
            k_new = dot(grads, q_head)
            v_new = dot(probs, g_head)
            key_term = k_new if key_term is None else key_term + k_new
            value_term = v_new if value_term is None else value_term + v_new
        kg_ref[:, cols] = key_term.astype(bf16)
        vg_ref[:, cols] = value_term.astype(bf16)
        out_pair = jnp.concatenate(out_t, 0).astype(bf16)
        att_t[pl.ds(start, PAIR), :] = out_pair
        att_ref[:, cols] = out_pair.T
        qg_ref[:, cols] = jnp.concatenate(qg_t, 0).astype(bf16).T
        return carry

    lax.fori_loop(0, HEADS // 2, pair_step, 0)

    normed_t = normed_all[...].T
    core = core_ref[0]

    def owner_rows(term):
        parts = [term[48 * m + 24 * low:48 * m + 24 * low + 24] for low in range(2) for m in range(16)]
        return jnp.concatenate(parts, 0).astype(bf16)

    for target, side in ((keep_ref, core), (send_ref, 1 - core)):
        cols = pl.ds(pl.multiple_of(side * SIDE, SIDE), SIDE)
        target[0] = owner_rows(dot(normed_t[:, :CELLS], qg_ref[:, cols]))
        target[1] = owner_rows(dot(normed_t, kg_ref[:, cols]))
        target[2] = owner_rows(dot(normed_t, vg_ref[:, cols]))
        target[3] = owner_rows(dot(att_t[...], dy_ref[:, cols]))


def attend_call(near, count, core, q, k, v, g, normed, lo, hi, anchors, dy, wk, wv):
    smem = pl.BlockSpec(memory_space=pltpu.SMEM)
    vmem = pl.BlockSpec(memory_space=pltpu.VMEM)
    return pl.pallas_call(
        attend_kernel,
        in_specs=[smem] * 3 + [vmem] * 11,
        out_shape=[
            jax.ShapeDtypeStruct((CELLS, D), bf16),
            jax.ShapeDtypeStruct((CELLS, D), bf16),
            jax.ShapeDtypeStruct((KEY_ROWS, D), bf16),
            jax.ShapeDtypeStruct((KEY_ROWS, D), bf16),
            jax.ShapeDtypeStruct((4, D, SIDE), bf16),
            jax.ShapeDtypeStruct((4, D, SIDE), bf16),
        ],
        scratch_shapes=[
            pltpu.VMEM((KEY_ROWS, D), bf16),
            pltpu.VMEM((KEY_ROWS, D), bf16),
            pltpu.VMEM((D, KEY_ROWS), bf16),
            pltpu.VMEM((D, KEY_ROWS), bf16),
            pltpu.VMEM((POOL_ROWS, CELLS), f32),
            pltpu.VMEM((D, CELLS), bf16),
            pltpu.VMEM((KEY_ROWS, D), bf16),
        ],
        compiler_params=params(48),
    )(near, count, core, q, k, v, g, normed, lo, hi, anchors, dy, wk, wv)


def back_kernel(x_ref, att_ref, qg_ref, kg_ref, vg_ref, wq_ref, wk_ref, wv_ref, wo_ref,
                mixed_ref, own_ref, lo_ref, hi_ref, an_ref):
    kv = dot(kg_ref[...], wk_ref[...], NT) + dot(vg_ref[...], wv_ref[...], NT)
    own_ref[...] = kv[:CELLS] + dot(qg_ref[...], wq_ref[...], NT)
    lo_ref[...] = kv[CELLS:CELLS + BS].astype(bf16)
    hi_ref[...] = kv[CELLS + BS:POOL_ROWS].astype(bf16)
    an_ref[...] = kv[POOL_ROWS:].astype(bf16)
    mixed_ref[...] = (x_ref[...].astype(f32) + dot(att_ref[...], wo_ref[...])).astype(bf16)


def back_call(x, att, qg, kg, vg, wq, wk, wv, wo):
    return pl.pallas_call(
        back_kernel,
        out_shape=[
            jax.ShapeDtypeStruct((CELLS, D), bf16),
            jax.ShapeDtypeStruct((CELLS, D), f32),
            jax.ShapeDtypeStruct((BS, D), bf16),
            jax.ShapeDtypeStruct((BS, D), bf16),
            jax.ShapeDtypeStruct((ANCHORS, D), bf16),
        ],
        compiler_params=params(40),
    )(x, att, qg, kg, vg, wq, wk, wv, wo)


def final_kernel(x_ref, dy_ref, own_ref, lo_ref, hi_ref, an_ref, anchor_ref, face_ref, out_ref):
    x = x_ref[...].astype(f32)
    inverse = lax.rsqrt(jnp.mean(x * x, axis=-1, keepdims=True) + EPSILON)

    def placed(index_row, rows):
        cells = lax.broadcasted_iota(jnp.int32, (CELLS, index_row.shape[1]), 0)
        return dot((cells == index_row).astype(bf16), rows)

    normed_grad = (
        own_ref[...]
        + placed(face_ref[0:1, :], lo_ref[...])
        + placed(face_ref[1:2, :], hi_ref[...])
        + placed(anchor_ref[...], an_ref[...])
    )
    cube = inverse * inverse * inverse
    out_ref[...] = (
        dy_ref[...].astype(f32)
        + inverse * normed_grad
        - x * cube * jnp.mean(normed_grad * x, axis=-1, keepdims=True)
    ).astype(bf16)


def final_call(x, dy, own, from_lo, from_hi, from_anchors, anchor_tiled, face_rows):
    return pl.pallas_call(
        final_kernel,
        out_shape=jax.ShapeDtypeStruct((CELLS, D), bf16),
        compiler_params=params(32),
    )(x, dy, own, from_lo, from_hi, from_anchors, anchor_tiled, face_rows)


PLANE = ("y", "xl", "xh")


def swapped(value, axis):
    return lax.ppermute(value, axis, [(0, 1), (1, 0)])


def shifted(value, axis, step):
    count = lax.axis_size(axis)
    return lax.ppermute(value, axis, [(i, (i + step) % count) for i in range(count)])


def along(value, step):
    count = 32
    pairs = [(i, i + step) for i in range(count) if 0 <= i + step < count]
    return lax.ppermute(value, ("z", "xl", "core"), pairs)


def reduced(keep, send):
    arrived = swapped(send, "core")
    both = (keep.astype(f32) + arrived.astype(f32)).astype(bf16)
    spread = lax.all_to_all(both.reshape(16, 192, SIDE), PLANE, 0, 0, tiled=True)
    plane = jnp.sum(spread.astype(f32), axis=0).astype(bf16)
    column = lax.all_to_all(plane.reshape(8, 24, SIDE), "z", 0, 0, tiled=True)
    rows = jnp.sum(column.astype(f32), axis=0).reshape(2, 12, SIDE)
    core = lax.axis_index("core")
    mine = lax.dynamic_index_in_dim(rows, core, 0, keepdims=False)
    other = swapped(lax.dynamic_index_in_dim(rows, 1 - core, 0, keepdims=False), "core")
    return jnp.where(
        core == 0,
        jnp.concatenate([mine, other], 1),
        jnp.concatenate([other, mine], 1),
    )


def body(
    cell_features,
    cotangent,
    query_weight,
    key_weight,
    value_weight,
    out_weight,
    anchor_index,
    face_cells,
    halo_count,
    neighbour_blocks,
):
    x = cell_features[0]
    dy = cotangent[0]
    face_rows = face_cells.reshape(2, BS)
    normed, sent_anchors, sent_lo, sent_hi = send_call(x, anchor_index, face_rows)
    from_lo = along(sent_hi, 1)
    from_hi = along(sent_lo, -1)
    column = jnp.concatenate(
        [sent_anchors] + [shifted(sent_anchors, "y", -k) for k in (1, 2, 3)], 0
    )
    anchors = jnp.concatenate([column, swapped(column, "xh")], 0)
    weights = (query_weight, key_weight, value_weight, out_weight)
    q, k, v, g = project_call(normed, dy, *weights)
    core = lax.axis_index("core").astype(jnp.int32).reshape(1)
    att, qg, kg, vg, keep, send = attend_call(
        neighbour_blocks.reshape(2, NB), halo_count.reshape(2), core, q, k, v, g,
        normed, from_lo, from_hi, anchors, dy, key_weight, value_weight,
    )
    mixed, own, to_lo, to_hi, to_anchors = back_call(x, att, qg, kg, vg, *weights)
    back_hi = along(to_lo, -1)
    back_lo = along(to_hi, 1)
    crossed = swapped(to_anchors[128:], "xh")
    shares = jnp.concatenate(
        [to_anchors[:128].reshape(4, 32, D), crossed.reshape(4, 32, D)], 1
    )
    back_anchors = jnp.concatenate(
        [shares[0]] + [shifted(shares[k], "y", k) for k in (1, 2, 3)], 0
    )
    cell_grad = final_call(
        x, dy, own, back_lo, back_hi, back_anchors, jnp.tile(anchor_index, (1, 8)), face_rows
    )
    weight_grads = reduced(keep, send)
    return mixed[None], cell_grad[None], weight_grads


def solution(mesh):
    fine = Mesh(mesh.devices.reshape(4, 2, 8, 2, 2), ("y", "xh", "z", "xl", "core"))
    dom = ("z", "xl", "core")
    blk = ("y", "xh")
    return jax.shard_map(
        body,
        mesh=fine,
        in_specs=(
            P(dom, blk, None),
            P(dom, blk, None),
            P(),
            P(),
            P(),
            P(),
            P(dom, blk),
            P(dom, blk, None, None),
            P(dom, blk, None),
            P(dom, blk, None),
        ),
        out_specs=(P(dom, blk, None), P(dom, blk, None), P(blk + dom, None)),
        check_vma=False,
    )
```

```python
import functools

import jax
import jax.numpy as jnp
from jax import lax
from jax.experimental import pallas as pl
from jax.experimental.pallas import tpu as pltpu
from jax.sharding import Mesh, PartitionSpec as P

HEADS = 12
BS = 128
NB = 3
D = 768
CELLS = 256
ANCHORS = 256
POOL_ROWS = 512
KEY_ROWS = 768
HEAD = 64
SIDE = 384
PAIRS = 3
VMEM_MIB = 48
PAIR = 128
SCALE = 0.125
EPSILON = 1e-06
MASKED = -1e30

f32 = jnp.float32
bf16 = jnp.bfloat16

NN = (((1,), (0,)), ((), ()))
NT = (((1,), (1,)), ((), ()))
TN = (((0,), (0,)), ((), ()))


def dot(a, b, dims=NN):
    return lax.dot_general(a, b, dims, preferred_element_type=f32)


def params():
    return pltpu.CompilerParams(vmem_limit_bytes=VMEM_MIB << 20)


def send_kernel(x_ref, anchor_ref, face_ref, normed_ref, rows_a_ref, rows_lo_ref, rows_hi_ref):
    x = x_ref[...].astype(f32)
    inverse = lax.rsqrt(jnp.mean(x * x, axis=-1, keepdims=True) + EPSILON)
    normed = (x * inverse).astype(bf16)
    normed_ref[...] = normed

    def picked(index_row):
        cells = lax.broadcasted_iota(jnp.int32, (CELLS, index_row.shape[1]), 0)
        one_hot = (cells == index_row).astype(bf16)
        return dot(one_hot, normed, TN).astype(bf16)

    rows_a_ref[...] = picked(anchor_ref[...])
    rows_lo_ref[...] = picked(face_ref[0:1, :])
    rows_hi_ref[...] = picked(face_ref[1:2, :])


def send_call(x, anchor_row, face_rows):
    shapes = [(CELLS, D), (32, D), (BS, D), (BS, D)]
    return pl.pallas_call(
        send_kernel,
        out_shape=[jax.ShapeDtypeStruct(s, bf16) for s in shapes],
        compiler_params=params(),
    )(x, anchor_row, face_rows)


def project_kernel(n_ref, dy_ref, wq_ref, wk_ref, wv_ref, wo_ref, q_ref, k_ref, v_ref, g_ref):
    normed = n_ref[...]
    q_ref[...] = (dot(normed, wq_ref[...]).astype(bf16) * SCALE).astype(bf16)
    k_ref[...] = dot(normed, wk_ref[...]).astype(bf16)
    v_ref[...] = dot(normed, wv_ref[...]).astype(bf16)
    g_ref[...] = dot(dy_ref[...], wo_ref[...], NT).astype(bf16)


def project_call(normed, dy, wq, wk, wv, wo):
    return pl.pallas_call(
        project_kernel,
        out_shape=[jax.ShapeDtypeStruct((CELLS, D), bf16)] * 4,
        compiler_params=params(),
    )(normed, dy, wq, wk, wv, wo)


def attend_kernel(extra, near_ref, count_ref, side_ref, q_ref, k_ref, v_ref, g_ref, n_ref, lo_ref,
                  hi_ref, an_ref, dy_ref, wk_ref, wv_ref, out_ref, keys, values, keys_t, values_t,
                  bias, outside):
    outside[0:BS, :] = lo_ref[...]
    outside[BS:2 * BS, :] = hi_ref[...]
    outside[2 * BS:, :] = an_ref[...]
    if extra:
        out_ref[1024:1024 + CELLS, :] = n_ref[...]
        out_ref[1024 + CELLS:1024 + KEY_ROWS, :] = outside[...]
        out_ref[1024 + KEY_ROWS:, :] = dy_ref[...]
    first = pl.multiple_of(side_ref[0] * SIDE, SIDE)
    mine = pl.ds(first, SIDE)
    keys[0:CELLS, :] = k_ref[:, mine]
    values[0:CELLS, :] = v_ref[:, mine]
    keys[CELLS:, :] = dot(outside[...], wk_ref[:, mine]).astype(bf16)
    values[CELLS:, :] = dot(outside[...], wv_ref[:, mine]).astype(bf16)
    keys_t[...] = keys[...].T
    values_t[...] = values[...].T

    row = lax.broadcasted_iota(jnp.int32, (BS, BS), 0)
    for block in range(4):
        for j in range(2):
            used = (near_ref[j, 0] == block) | (near_ref[j, 1] == block) | (near_ref[j, 2] == block)
            live = jnp.where(used, BS if block < 2 else count_ref[max(block - 2, 0)], 0)
            bias[block * BS:(block + 1) * BS, j * BS:(j + 1) * BS] = jnp.where(row < live, 0.0, MASKED)

    lane = lax.broadcasted_iota(jnp.int32, (CELLS, PAIR), 1)

    def softmax(scores):
        highest = jnp.max(scores, axis=0, keepdims=True)
        powers = jnp.exp(scores - highest)
        return powers * (1.0 / jnp.sum(powers, axis=0, keepdims=True))

    def score_grad(probs, prob_grad):
        weighted = probs * prob_grad
        return weighted - probs * jnp.sum(weighted, axis=0, keepdims=True)

    for pair in range(PAIRS):
        cols = slice(pair * PAIR, (pair + 1) * PAIR)
        k_pair = keys[:, cols]
        v_pair = values[:, cols]
        from_cols = pl.ds(pl.multiple_of(first + pair * PAIR, PAIR), PAIR)
        q_pair = q_ref[:, from_cols]
        g_pair = g_ref[:, from_cols]
        key_term = None
        value_term = None
        out_t = []
        qg_t = []
        for half in range(2):
            chosen = (lane >= HEAD) if half else (lane < HEAD)
            q_head = jnp.where(chosen, q_pair, jnp.zeros_like(q_pair))
            g_head = jnp.where(chosen, g_pair, jnp.zeros_like(g_pair))
            scores = dot(k_pair, q_head, NT)
            prob_grad = dot(v_pair, g_head, NT)
            near = softmax(scores[:POOL_ROWS] + bias[...])
            anchor = softmax(scores[POOL_ROWS:])
            probs = jnp.concatenate([near.astype(bf16), anchor.astype(bf16)], 0)
            grads = jnp.concatenate(
                [
                    score_grad(near, prob_grad[:POOL_ROWS]).astype(bf16),
                    score_grad(anchor, prob_grad[POOL_ROWS:]).astype(bf16),
                ],
                0,
            )
            head_rows = slice(pair * PAIR + half * HEAD, pair * PAIR + (half + 1) * HEAD)
            out_t.append(dot(values_t[head_rows, :], probs))
            qg_t.append(dot(keys_t[head_rows, :], grads) * SCALE)
            k_new = dot(grads, q_head)
            v_new = dot(probs, g_head)
            key_term = k_new if key_term is None else key_term + k_new
            value_term = v_new if value_term is None else value_term + v_new
        shifted_cols = slice(SIDE + pair * PAIR, SIDE + (pair + 1) * PAIR)
        out_ref[CELLS:CELLS + KEY_ROWS, cols] = key_term.astype(bf16)
        out_ref[CELLS:CELLS + KEY_ROWS, shifted_cols] = value_term.astype(bf16)
        out_ref[0:CELLS, cols] = jnp.concatenate(out_t, 0).astype(bf16).T
        out_ref[0:CELLS, shifted_cols] = jnp.concatenate(qg_t, 0).astype(bf16).T


def attend_call(extra, near, count, side, q, k, v, g, normed, lo, hi, anchors, dy, wk, wv):
    smem = pl.BlockSpec(memory_space=pltpu.SMEM)
    vmem = pl.BlockSpec(memory_space=pltpu.VMEM)
    return pl.pallas_call(
        functools.partial(attend_kernel, extra),
        in_specs=[smem] * 3 + [vmem] * 11,
        out_shape=jax.ShapeDtypeStruct((2048 if extra else 1024, D), bf16),
        scratch_shapes=[
            pltpu.VMEM((KEY_ROWS, SIDE), bf16),
            pltpu.VMEM((KEY_ROWS, SIDE), bf16),
            pltpu.VMEM((SIDE, KEY_ROWS), bf16),
            pltpu.VMEM((SIDE, KEY_ROWS), bf16),
            pltpu.VMEM((POOL_ROWS, CELLS), f32),
            pltpu.VMEM((POOL_ROWS, D), bf16),
        ],
        compiler_params=params(),
    )(near, count, side, q, k, v, g, normed, lo, hi, anchors, dy, wk, wv)


def outer_kernel(place_ref, first_ref, own_ref, got_ref, *refs):
    to_x, to_y, (normed_t, parts) = refs[0:4], refs[4:8], refs[8:]
    normed_t[:, :KEY_ROWS] = first_ref[1024:1024 + KEY_ROWS, :].T
    normed_t[:, KEY_ROWS:] = got_ref[1024:1024 + KEY_ROWS, :].T

    def block(term, low, cols):
        rows = [term[m + 24 * low:m + 24 * low + 24, cols] for m in range(0, term.shape[0], 48)]
        return jnp.concatenate(rows, 0).astype(bf16)

    def keep(matrix, term, cols):
        for high in range(2):
            for low in range(2):
                parts[matrix, 2 * high + low] = block(term[high * SIDE:(high + 1) * SIDE], low, cols)

    left, right = slice(0, SIDE), slice(SIDE, D)
    keep(0, dot(normed_t[:, :CELLS], own_ref[0:CELLS, right])
         + dot(normed_t[:, KEY_ROWS:KEY_ROWS + CELLS], got_ref[0:CELLS, right]), slice(None))
    pairs = (
        dot(normed_t[:, :KEY_ROWS], own_ref[CELLS:1024, :])
        + dot(normed_t[:, KEY_ROWS:], got_ref[CELLS:1024, :])
    )
    keep(1, pairs, left)
    keep(2, pairs, right)
    out_term = dot(own_ref[0:CELLS, left], first_ref[1024 + KEY_ROWS:, :], TN) + dot(
        got_ref[0:CELLS, left], got_ref[1024 + KEY_ROWS:, :], TN
    )
    for high in range(2):
        for low in range(2):
            parts[3, 2 * high + low] = block(out_term, low, right if high else left)
    x_place, y_place = place_ref[0], place_ref[1]
    for step in range(4):
        x_slot = (x_place + step) % 4
        y_slot = (y_place + step) % 4
        for index in range(4):
            to_x[step][index] = parts[index, x_slot, 0:96, :]
            to_y[step][index] = parts[y_slot, index, 96:192, :]


def outer_call(place, first, own, got):
    smem = pl.BlockSpec(memory_space=pltpu.SMEM)
    vmem = pl.BlockSpec(memory_space=pltpu.VMEM)
    return pl.pallas_call(
        outer_kernel,
        in_specs=[smem] + [vmem] * 3,
        out_shape=[jax.ShapeDtypeStruct((4, 96, SIDE), bf16)] * 8,
        scratch_shapes=[pltpu.VMEM((D, 2 * KEY_ROWS), bf16), pltpu.VMEM((4, 4, 192, SIDE), bf16)],
        compiler_params=params(),
    )(place, first, own, got)


def second_kernel(place_ref, *refs):
    from_x, from_y, to_y, to_x = refs[0:4], refs[4:8], refs[8:12], refs[12:16]
    x_place, y_place = place_ref[0], place_ref[1]

    def total(arrays, slot):
        return (
            arrays[0][slot].astype(f32) + arrays[1][slot].astype(f32)
            + arrays[2][slot].astype(f32) + arrays[3][slot].astype(f32)
        ).astype(bf16)

    for step in range(4):
        to_y[step][...] = total(from_x, (y_place + step) % 4)
        to_x[step][...] = total(from_y, (x_place + step) % 4)


def second_call(place, arrays):
    smem = pl.BlockSpec(memory_space=pltpu.SMEM)
    vmem = pl.BlockSpec(memory_space=pltpu.VMEM)
    return pl.pallas_call(
        second_kernel,
        in_specs=[smem] + [vmem] * 8,
        out_shape=[jax.ShapeDtypeStruct((96, SIDE), bf16)] * 8,
        compiler_params=params(),
    )(place, *arrays)


def third_kernel(place_ref, *refs):
    from_y, from_x, outs, parts = refs[0:4], refs[4:8], refs[8:16], refs[16]
    low = sum(r[...].astype(f32) for r in from_y)
    high = sum(r[...].astype(f32) for r in from_x)
    for z in range(4):
        parts[z] = low[24 * z:24 * z + 24]
        parts[4 + z] = high[24 * z:24 * z + 24]
    z_place = place_ref[2]
    for step in range(8):
        outs[step][...] = parts[(z_place + step) % 8].astype(bf16)


def third_call(place, arrays):
    smem = pl.BlockSpec(memory_space=pltpu.SMEM)
    vmem = pl.BlockSpec(memory_space=pltpu.VMEM)
    return pl.pallas_call(
        third_kernel,
        in_specs=[smem] + [vmem] * 8,
        out_shape=[jax.ShapeDtypeStruct((24, SIDE), bf16)] * 8,
        scratch_shapes=[pltpu.VMEM((8, 24, SIDE), f32)],
        compiler_params=params(),
    )(place, *arrays)


def back_kernel(core_ref, x_ref, first_ref, own_ref, wq_ref, wk_ref, wv_ref, wo_ref,
                mixed_ref, ng_ref, lo_ref, hi_ref, an_ref):
    core = core_ref[0]
    kv = None
    extra = None
    out = x_ref[...].astype(f32)
    for source, side in ((own_ref, core), (first_ref, 1 - core)):
        half = pl.ds(pl.multiple_of(side * SIDE, SIDE), SIDE)
        term = dot(source[CELLS:1024, :SIDE], wk_ref[:, half], NT)
        kv = term if kv is None else kv + term
        kv = kv + dot(source[CELLS:1024, SIDE:], wv_ref[:, half], NT)
        term = dot(source[0:CELLS, SIDE:], wq_ref[:, half], NT)
        extra = term if extra is None else extra + term
        out = out + dot(source[0:CELLS, :SIDE], wo_ref[half, :])
    ng_ref[...] = kv[:CELLS] + extra
    lo_ref[...] = kv[CELLS:CELLS + BS].astype(bf16)
    hi_ref[...] = kv[CELLS + BS:POOL_ROWS].astype(bf16)
    an_ref[...] = kv[POOL_ROWS:].astype(bf16)
    mixed_ref[...] = out.astype(bf16)


def back_call(core, x, first, own, wq, wk, wv, wo):
    smem = pl.BlockSpec(memory_space=pltpu.SMEM)
    vmem = pl.BlockSpec(memory_space=pltpu.VMEM)
    return pl.pallas_call(
        back_kernel,
        in_specs=[smem] + [vmem] * 7,
        out_shape=[
            jax.ShapeDtypeStruct((CELLS, D), bf16),
            jax.ShapeDtypeStruct((CELLS, D), f32),
            jax.ShapeDtypeStruct((BS, D), bf16),
            jax.ShapeDtypeStruct((BS, D), bf16),
            jax.ShapeDtypeStruct((ANCHORS, D), bf16),
        ],
        compiler_params=params(),
    )(core, x, first, own, wq, wk, wv, wo)


def final_kernel(x_ref, dy_ref, own_ref, lo_ref, hi_ref, an_ref, anchor_ref, face_ref, out_ref):
    x = x_ref[...].astype(f32)
    inverse = lax.rsqrt(jnp.mean(x * x, axis=-1, keepdims=True) + EPSILON)

    def placed(index_row, rows):
        cells = lax.broadcasted_iota(jnp.int32, (CELLS, index_row.shape[1]), 0)
        return dot((cells == index_row).astype(bf16), rows)

    normed_grad = (
        own_ref[...]
        + placed(face_ref[0:1, :], lo_ref[...])
        + placed(face_ref[1:2, :], hi_ref[...])
        + placed(anchor_ref[...], an_ref[...])
    )
    cube = inverse * inverse * inverse
    out_ref[...] = (
        dy_ref[...].astype(f32)
        + inverse * normed_grad
        - x * cube * jnp.mean(normed_grad * x, axis=-1, keepdims=True)
    ).astype(bf16)


def final_call(x, dy, own, from_lo, from_hi, from_anchors, anchor_tiled, face_rows):
    return pl.pallas_call(
        final_kernel,
        out_shape=jax.ShapeDtypeStruct((CELLS, D), bf16),
        compiler_params=params(),
    )(x, dy, own, from_lo, from_hi, from_anchors, anchor_tiled, face_rows)


def swapped(value, axis):
    return lax.ppermute(value, axis, [(0, 1), (1, 0)])


def shifted(value, axis, step):
    count = lax.axis_size(axis)
    return lax.ppermute(value, axis, [(i, (i + step) % count) for i in range(count)])


def along(value, step):
    count = 32
    pairs = [(i, i + step) for i in range(count) if 0 <= i + step < count]
    return lax.ppermute(value, ("z", "xl", "core"), pairs)


X_AXIS = ("xh", "xl")


def spread(arrays, axis):
    return [arrays[0]] + [shifted(arrays[k], axis, k) for k in range(1, len(arrays))]


def settled(rows):
    pieces = rows.reshape(2, 12, SIDE)
    y, xh, core = (lax.axis_index(a) for a in ("y", "xh", "core"))
    last = y == 3
    pick = jnp.where(last, xh, core)
    own = lax.dynamic_index_in_dim(pieces, pick, 0, keepdims=False)
    other = lax.dynamic_index_in_dim(pieces, 1 - pick, 0, keepdims=False)

    def device(y_at, xh_at, core_at):
        return (y_at * 2 + xh_at) * 2 + core_at

    turn, swap = [], []
    for h in range(2):
        for r in range(2):
            turn.append((device(3, h, r), device(3, r, h)))
            swap.append((device(3, h, r), device(3, r, 1 - h)))
            swap += [(device(m, h, r), device(m, h, 1 - r)) for m in range(3)]
    axes = ("y", "xh", "core")
    turned = lax.ppermute(own, axes, turn)
    here = jnp.where(last, turned, own)
    there = lax.ppermute(other, axes, swap)
    return jnp.where(
        core == 0, jnp.concatenate([here, there], 1), jnp.concatenate([there, here], 1)
    )


def body(
    cell_features,
    cotangent,
    query_weight,
    key_weight,
    value_weight,
    out_weight,
    anchor_index,
    face_cells,
    halo_count,
    neighbour_blocks,
):
    x = cell_features[0]
    dy = cotangent[0]
    face_rows = face_cells.reshape(2, BS)
    near = neighbour_blocks.reshape(2, NB)
    count = halo_count.reshape(2)
    weights = (query_weight, key_weight, value_weight, out_weight)
    axis = {a: lax.axis_index(a).astype(jnp.int32) for a in ("y", "xh", "z", "xl", "core")}
    core = axis["core"].reshape(1)
    place = jnp.stack([axis["xh"] * 2 + axis["xl"], axis["y"], axis["z"]])

    normed, sent_anchors, sent_lo, sent_hi = send_call(x, anchor_index, face_rows)
    both = jnp.concatenate([sent_anchors, swapped(sent_anchors, "xh")], 0)
    from_lo = along(sent_hi, 1)
    from_hi = along(sent_lo, -1)
    anchors = jnp.concatenate([both] + [shifted(both, "y", -k) for k in (1, 2, 3)], 0)
    q, k, v, g = project_call(normed, dy, *weights)

    common = (q, k, v, g, normed, from_lo, from_hi, anchors, dy, key_weight, value_weight)
    first = attend_call(True, near, count, 1 - core, *common)
    got = swapped(first, "core")
    own = attend_call(False, near, count, core, *common)

    sums = outer_call(place, first, own, got)
    sums = spread(sums[:4], X_AXIS) + spread(sums[4:], "y")
    mixed, own_grad, to_lo, to_hi, to_anchors = back_call(core, x, first, own, *weights)
    sums = second_call(place, sums)
    sums = spread(sums[:4], "y") + spread(sums[4:], X_AXIS)
    sums = spread(third_call(place, sums), "z")
    rows = sum(s.astype(f32) for s in sums)
    weight_grads = settled(rows)

    back_hi = along(to_lo, -1)
    back_lo = along(to_hi, 1)
    shares = to_anchors.reshape(4, 64, D)
    shares = [shares[0]] + [shifted(shares[k], "y", k) for k in (1, 2, 3)]
    crossed = swapped(jnp.concatenate([s[32:] for s in shares], 0), "xh")
    back_anchors = jnp.concatenate([s[:32] for s in shares] + [crossed], 0)
    cell_grad = final_call(
        x, dy, own_grad, back_lo, back_hi, back_anchors, jnp.tile(anchor_index, (1, 8)), face_rows
    )
    return mixed[None], cell_grad[None], weight_grads


def solution(mesh):
    fine = Mesh(mesh.devices.reshape(4, 2, 8, 2, 2), ("y", "xh", "z", "xl", "core"))
    dom = ("z", "xl", "core")
    blk = ("y", "xh")
    return jax.shard_map(
        body,
        mesh=fine,
        in_specs=(
            P(dom, blk, None),
            P(dom, blk, None),
            P(),
            P(),
            P(),
            P(),
            P(dom, blk),
            P(dom, blk, None, None),
            P(dom, blk, None),
            P(dom, blk, None),
        ),
        out_specs=(P(dom, blk, None), P(dom, blk, None), P(blk + dom, None)),
        check_vma=False,
    )
```

```python
import functools

import jax
import jax.numpy as jnp
from jax import lax
from jax.experimental import pallas as pl
from jax.experimental.pallas import tpu as pltpu
from jax.sharding import Mesh, PartitionSpec as P

HEADS = 12
BS = 128
NB = 3
D = 768
CELLS = 256
ANCHORS = 256
POOL_ROWS = 512
KEY_ROWS = 768
HEAD = 64
SIDE = 384
PAIRS = 3
OTHERS = 7
PAIR = 128
SCALE = 0.125
EPSILON = 1e-06
MASKED = -1e30

f32 = jnp.float32
bf16 = jnp.bfloat16

NN = (((1,), (0,)), ((), ()))
NT = (((1,), (1,)), ((), ()))
TN = (((0,), (0,)), ((), ()))


def dot(a, b, dims=NN):
    return lax.dot_general(a, b, dims, preferred_element_type=f32)


def params(mib):
    return pltpu.CompilerParams(vmem_limit_bytes=mib << 20)


def send_kernel(x_ref, anchor_ref, face_ref, normed_ref, rows_a_ref, rows_lo_ref, rows_hi_ref):
    x = x_ref[...].astype(f32)
    inverse = lax.rsqrt(jnp.mean(x * x, axis=-1, keepdims=True) + EPSILON)
    normed = (x * inverse).astype(bf16)
    normed_ref[...] = normed

    def picked(index_row):
        cells = lax.broadcasted_iota(jnp.int32, (CELLS, index_row.shape[1]), 0)
        one_hot = (cells == index_row).astype(bf16)
        return dot(one_hot, normed, TN).astype(bf16)

    rows_a_ref[...] = picked(anchor_ref[...])
    rows_lo_ref[...] = picked(face_ref[0:1, :])
    rows_hi_ref[...] = picked(face_ref[1:2, :])


def send_call(x, anchor_row, face_rows):
    shapes = [(CELLS, D), (32, D), (BS, D), (BS, D)]
    return pl.pallas_call(
        send_kernel,
        out_shape=[jax.ShapeDtypeStruct(s, bf16) for s in shapes],
        compiler_params=params(8),
    )(x, anchor_row, face_rows)


def project_kernel(n_ref, dy_ref, wq_ref, wk_ref, wv_ref, wo_ref, q_ref, k_ref, v_ref, g_ref):
    normed = n_ref[...]
    q_ref[...] = (dot(normed, wq_ref[...]).astype(bf16) * SCALE).astype(bf16)
    k_ref[...] = dot(normed, wk_ref[...]).astype(bf16)
    v_ref[...] = dot(normed, wv_ref[...]).astype(bf16)
    g_ref[...] = dot(dy_ref[...], wo_ref[...], NT).astype(bf16)


def project_call(normed, dy, wq, wk, wv, wo):
    return pl.pallas_call(
        project_kernel,
        out_shape=[jax.ShapeDtypeStruct((CELLS, D), bf16)] * 4,
        compiler_params=params(14),
    )(normed, dy, wq, wk, wv, wo)


def attend_kernel(extra, near_ref, count_ref, side_ref, q_ref, k_ref, v_ref, g_ref, n_ref, lo_ref,
                  hi_ref, dy_ref, wk_ref, wv_ref, *refs):
    anchor_refs = refs[:OTHERS + 1]
    out_ref, keys, values, keys_t, values_t, bias, outside = refs[OTHERS + 1:]
    outside[0:BS, :] = lo_ref[...]
    outside[BS:2 * BS, :] = hi_ref[...]
    for index, rows in enumerate(anchor_refs):
        outside[2 * BS + 32 * index:2 * BS + 32 * index + 32, :] = rows[...]
    if extra:
        out_ref[1024:1024 + KEY_ROWS, :CELLS] = n_ref[...].T
        out_ref[1024:1024 + KEY_ROWS, CELLS:] = outside[...].T
        out_ref[1024 + KEY_ROWS:, :] = dy_ref[...]
    first = pl.multiple_of(side_ref[0] * SIDE, SIDE)
    mine = pl.ds(first, SIDE)
    keys[0:CELLS, :] = k_ref[:, mine]
    values[0:CELLS, :] = v_ref[:, mine]
    keys[CELLS:, :] = dot(outside[...], wk_ref[:, mine]).astype(bf16)
    values[CELLS:, :] = dot(outside[...], wv_ref[:, mine]).astype(bf16)
    keys_t[...] = keys[...].T
    values_t[...] = values[...].T

    row = lax.broadcasted_iota(jnp.int32, (BS, BS), 0)
    for block in range(4):
        for j in range(2):
            used = (near_ref[j, 0] == block) | (near_ref[j, 1] == block) | (near_ref[j, 2] == block)
            live = jnp.where(used, BS if block < 2 else count_ref[max(block - 2, 0)], 0)
            bias[block * BS:(block + 1) * BS, j * BS:(j + 1) * BS] = jnp.where(row < live, 0.0, MASKED)

    lane = lax.broadcasted_iota(jnp.int32, (CELLS, PAIR), 1)

    def softmax(scores):
        highest = jnp.max(scores, axis=0, keepdims=True)
        powers = jnp.exp(scores - highest)
        return powers * (1.0 / jnp.sum(powers, axis=0, keepdims=True))

    def score_grad(probs, prob_grad):
        weighted = probs * prob_grad
        return weighted - probs * jnp.sum(weighted, axis=0, keepdims=True)

    for pair in range(PAIRS):
        cols = slice(pair * PAIR, (pair + 1) * PAIR)
        k_pair = keys[:, cols]
        v_pair = values[:, cols]
        from_cols = pl.ds(pl.multiple_of(first + pair * PAIR, PAIR), PAIR)
        q_pair = q_ref[:, from_cols]
        g_pair = g_ref[:, from_cols]
        key_term = None
        value_term = None
        out_t = []
        qg_t = []
        for half in range(2):
            chosen = (lane >= HEAD) if half else (lane < HEAD)
            q_head = jnp.where(chosen, q_pair, jnp.zeros_like(q_pair))
            g_head = jnp.where(chosen, g_pair, jnp.zeros_like(g_pair))
            scores = dot(k_pair, q_head, NT)
            prob_grad = dot(v_pair, g_head, NT)
            near = softmax(scores[:POOL_ROWS] + bias[...])
            anchor = softmax(scores[POOL_ROWS:])
            probs = jnp.concatenate([near.astype(bf16), anchor.astype(bf16)], 0)
            grads = jnp.concatenate(
                [
                    score_grad(near, prob_grad[:POOL_ROWS]).astype(bf16),
                    score_grad(anchor, prob_grad[POOL_ROWS:]).astype(bf16),
                ],
                0,
            )
            head_rows = slice(pair * PAIR + half * HEAD, pair * PAIR + (half + 1) * HEAD)
            out_t.append(dot(values_t[head_rows, :], probs))
            qg_t.append(dot(keys_t[head_rows, :], grads) * SCALE)
            k_new = dot(grads, q_head)
            v_new = dot(probs, g_head)
            key_term = k_new if key_term is None else key_term + k_new
            value_term = v_new if value_term is None else value_term + v_new
        shifted_cols = slice(SIDE + pair * PAIR, SIDE + (pair + 1) * PAIR)
        out_ref[CELLS:CELLS + KEY_ROWS, cols] = key_term.astype(bf16)
        out_ref[CELLS:CELLS + KEY_ROWS, shifted_cols] = value_term.astype(bf16)
        out_ref[0:CELLS, cols] = jnp.concatenate(out_t, 0).astype(bf16).T
        out_ref[0:CELLS, shifted_cols] = jnp.concatenate(qg_t, 0).astype(bf16).T


def attend_call(extra, near, count, side, q, k, v, g, normed, lo, hi, dy, wk, wv, anchors):
    smem = pl.BlockSpec(memory_space=pltpu.SMEM)
    vmem = pl.BlockSpec(memory_space=pltpu.VMEM)
    return pl.pallas_call(
        functools.partial(attend_kernel, extra),
        in_specs=[smem] * 3 + [vmem] * (11 + OTHERS),
        out_shape=jax.ShapeDtypeStruct((2048 if extra else 1024, D), bf16),
        scratch_shapes=[
            pltpu.VMEM((KEY_ROWS, SIDE), bf16),
            pltpu.VMEM((KEY_ROWS, SIDE), bf16),
            pltpu.VMEM((SIDE, KEY_ROWS), bf16),
            pltpu.VMEM((SIDE, KEY_ROWS), bf16),
            pltpu.VMEM((POOL_ROWS, CELLS), f32),
            pltpu.VMEM((POOL_ROWS, D), bf16),
        ],
        compiler_params=params(24),
    )(near, count, side, q, k, v, g, normed, lo, hi, dy, wk, wv, *anchors)


def outer_kernel(first_ref, own_ref, got_ref, parts):
    mine = slice(1024, 1024 + KEY_ROWS)

    def block(term, low, cols):
        rows = [term[m + 24 * low:m + 24 * low + 24, cols] for m in range(0, term.shape[0], 48)]
        return jnp.concatenate(rows, 0).astype(bf16)

    def keep(matrix, term, cols):
        for high in range(2):
            for low in range(2):
                parts[4 * matrix + 2 * high + low] = block(term[high * SIDE:(high + 1) * SIDE], low, cols)

    left, right = slice(0, SIDE), slice(SIDE, D)
    keep(0, dot(first_ref[mine, :CELLS], own_ref[0:CELLS, right])
         + dot(got_ref[mine, :CELLS], got_ref[0:CELLS, right]), slice(None))
    pairs = (
        dot(first_ref[mine, :], own_ref[CELLS:1024, :])
        + dot(got_ref[mine, :], got_ref[CELLS:1024, :])
    )
    keep(1, pairs, left)
    keep(2, pairs, right)
    out_term = dot(own_ref[0:CELLS, left], first_ref[1024 + KEY_ROWS:, :], TN) + dot(
        got_ref[0:CELLS, left], got_ref[1024 + KEY_ROWS:, :], TN
    )
    for high in range(2):
        for low in range(2):
            parts[12 + 2 * high + low] = block(out_term, low, right if high else left)

def outer_call(first, own, got):
    return pl.pallas_call(
        outer_kernel,
        out_shape=jax.ShapeDtypeStruct((16, 192, SIDE), bf16),
        compiler_params=params(24),
    )(first, own, got)


def plane_kernel(got_ref, out_ref):
    total = got_ref[0].astype(f32)
    for index in range(1, 16):
        total = total + got_ref[index].astype(f32)
    for z in range(8):
        out_ref[z] = total[24 * z:24 * z + 24].astype(bf16)


def plane_call(got):
    return pl.pallas_call(
        plane_kernel,
        out_shape=jax.ShapeDtypeStruct((8, 24, SIDE), bf16),
        compiler_params=params(10),
    )(got)


def back_kernel(core_ref, x_ref, first_ref, own_ref, wq_ref, wk_ref, wv_ref, wo_ref,
                mixed_ref, ng_ref, lo_ref, hi_ref, *anchor_refs):
    core = core_ref[0]
    kv = None
    extra = None
    out = x_ref[...].astype(f32)
    for source, side in ((own_ref, core), (first_ref, 1 - core)):
        half = pl.ds(pl.multiple_of(side * SIDE, SIDE), SIDE)
        term = dot(source[CELLS:1024, :SIDE], wk_ref[:, half], NT)
        kv = term if kv is None else kv + term
        kv = kv + dot(source[CELLS:1024, SIDE:], wv_ref[:, half], NT)
        term = dot(source[0:CELLS, SIDE:], wq_ref[:, half], NT)
        extra = term if extra is None else extra + term
        out = out + dot(source[0:CELLS, :SIDE], wo_ref[half, :])
    ng_ref[...] = kv[:CELLS] + extra
    lo_ref[...] = kv[CELLS:CELLS + BS].astype(bf16)
    hi_ref[...] = kv[CELLS + BS:POOL_ROWS].astype(bf16)
    for index, rows in enumerate(anchor_refs):
        rows[...] = kv[POOL_ROWS + 32 * index:POOL_ROWS + 32 * index + 32].astype(bf16)
    mixed_ref[...] = out.astype(bf16)


def back_call(core, x, first, own, wq, wk, wv, wo):
    smem = pl.BlockSpec(memory_space=pltpu.SMEM)
    vmem = pl.BlockSpec(memory_space=pltpu.VMEM)
    return pl.pallas_call(
        back_kernel,
        in_specs=[smem] + [vmem] * 7,
        out_shape=[
            jax.ShapeDtypeStruct((CELLS, D), bf16),
            jax.ShapeDtypeStruct((CELLS, D), f32),
            jax.ShapeDtypeStruct((BS, D), bf16),
            jax.ShapeDtypeStruct((BS, D), bf16),
        ] + [jax.ShapeDtypeStruct((32, D), bf16)] * (OTHERS + 1),
        compiler_params=params(24),
    )(core, x, first, own, wq, wk, wv, wo)


def final_kernel(x_ref, dy_ref, own_ref, lo_ref, hi_ref, anchor_ref, face_ref, *refs):
    rows_refs, out_ref = refs[:-1], refs[-1]
    x = x_ref[...].astype(f32)
    inverse = lax.rsqrt(jnp.mean(x * x, axis=-1, keepdims=True) + EPSILON)

    def placed(index_row, rows):
        cells = lax.broadcasted_iota(jnp.int32, (CELLS, index_row.shape[1]), 0)
        return dot((cells == index_row).astype(bf16), rows)

    shares = sum(rows[...].astype(f32) for rows in rows_refs)
    high = shares.astype(bf16)
    low = (shares - high.astype(f32)).astype(bf16)
    normed_grad = (
        own_ref[...]
        + placed(face_ref[0:1, :], lo_ref[...])
        + placed(face_ref[1:2, :], hi_ref[...])
        + placed(anchor_ref[...], high)
        + placed(anchor_ref[...], low)
    )
    cube = inverse * inverse * inverse
    out_ref[...] = (
        dy_ref[...].astype(f32)
        + inverse * normed_grad
        - x * cube * jnp.mean(normed_grad * x, axis=-1, keepdims=True)
    ).astype(bf16)


def final_call(x, dy, own, from_lo, from_hi, anchor_row, face_rows, shares):
    return pl.pallas_call(
        final_kernel,
        out_shape=jax.ShapeDtypeStruct((CELLS, D), bf16),
        compiler_params=params(12),
    )(x, dy, own, from_lo, from_hi, anchor_row, face_rows, *shares)


def swapped(value, axis):
    return lax.ppermute(value, axis, [(0, 1), (1, 0)])


def along(value, step):
    count = 32
    pairs = [(i, i + step) for i in range(count) if 0 <= i + step < count]
    return lax.ppermute(value, ("z", "xl", "core"), pairs)


SLOT_STEPS = [(dy, dx) for dy in range(4) for dx in range(2) if (dy, dx) != (0, 0)]
PLANE = ("y", "xh", "xl")


def to_slot(value, dy, dx):
    pairs = [
        (2 * y + h, 2 * ((y + dy) % 4) + (h + dx) % 2) for y in range(4) for h in range(2)
    ]
    return lax.ppermute(value, ("y", "xh"), pairs)


def settled(rows):
    pieces = rows.reshape(2, 12, SIDE)
    y, xh, core = (lax.axis_index(a) for a in ("y", "xh", "core"))
    last = y == 3
    pick = jnp.where(last, xh, core)
    own = lax.dynamic_index_in_dim(pieces, pick, 0, keepdims=False)
    other = lax.dynamic_index_in_dim(pieces, 1 - pick, 0, keepdims=False)

    def device(y_at, xh_at, core_at):
        return (y_at * 2 + xh_at) * 2 + core_at

    turn, swap = [], []
    for h in range(2):
        for r in range(2):
            turn.append((device(3, h, r), device(3, r, h)))
            swap.append((device(3, h, r), device(3, r, 1 - h)))
            swap += [(device(m, h, r), device(m, h, 1 - r)) for m in range(3)]
    axes = ("y", "xh", "core")
    turned = lax.ppermute(own, axes, turn)
    here = jnp.where(last, turned, own)
    there = lax.ppermute(other, axes, swap)
    return jnp.where(
        core == 0, jnp.concatenate([here, there], 1), jnp.concatenate([there, here], 1)
    )


def body(
    cell_features,
    cotangent,
    query_weight,
    key_weight,
    value_weight,
    out_weight,
    anchor_index,
    face_cells,
    halo_count,
    neighbour_blocks,
):
    x = cell_features[0]
    dy = cotangent[0]
    face_rows = face_cells.reshape(2, BS)
    near = neighbour_blocks.reshape(2, NB)
    count = halo_count.reshape(2)
    weights = (query_weight, key_weight, value_weight, out_weight)
    core = lax.axis_index("core").astype(jnp.int32).reshape(1)

    normed, sent_anchors, sent_lo, sent_hi = send_call(x, anchor_index, face_rows)
    anchors = [sent_anchors] + [to_slot(sent_anchors, -dy, dx) for dy, dx in SLOT_STEPS]
    from_lo = along(sent_hi, 1)
    from_hi = along(sent_lo, -1)
    q, k, v, g = project_call(normed, dy, *weights)

    common = (q, k, v, g, normed, from_lo, from_hi, dy, key_weight, value_weight, anchors)
    first = attend_call(True, near, count, 1 - core, *common)
    got = swapped(first, "core")
    own = attend_call(False, near, count, core, *common)

    parts = outer_call(first, own, got)
    plane = lax.all_to_all(parts, PLANE, 0, 0, tiled=True)
    column = lax.all_to_all(plane_call(plane), "z", 0, 0, tiled=True)
    weight_grads = settled(jnp.sum(column.astype(f32), axis=0))

    mixed, own_grad, to_lo, to_hi, *shares = back_call(core, x, first, own, *weights)
    back_hi = along(to_lo, -1)
    back_lo = along(to_hi, 1)
    shares = [shares[0]] + [
        to_slot(share, dy, dx) for share, (dy, dx) in zip(shares[1:], SLOT_STEPS)
    ]
    cell_grad = final_call(x, dy, own_grad, back_lo, back_hi, anchor_index, face_rows, shares)
    return mixed[None], cell_grad[None], weight_grads


def solution(mesh):
    fine = Mesh(mesh.devices.reshape(4, 2, 8, 2, 2), ("y", "xh", "z", "xl", "core"))
    dom = ("z", "xl", "core")
    blk = ("y", "xh")
    return jax.shard_map(
        body,
        mesh=fine,
        in_specs=(
            P(dom, blk, None),
            P(dom, blk, None),
            P(),
            P(),
            P(),
            P(),
            P(dom, blk),
            P(dom, blk, None, None),
            P(dom, blk, None),
            P(dom, blk, None),
        ),
        out_specs=(P(dom, blk, None), P(dom, blk, None), P(blk + dom, None)),
        check_vma=False,
    )
```

```python
import functools

import jax
import jax.numpy as jnp
from jax import lax
from jax.experimental import pallas as pl
from jax.experimental.pallas import tpu as pltpu
from jax.sharding import Mesh, PartitionSpec as P

HEADS = 12
BS = 128
NB = 3
D = 768
CELLS = 256
ANCHORS = 256
POOL_ROWS = 512
KEY_ROWS = 768
HEAD = 64
SIDE = 384
PAIRS = 3
SLOTS = 8
PAIR = 128
SCALE = 0.125
EPSILON = 1e-06
MASKED = -1e30

f32 = jnp.float32
bf16 = jnp.bfloat16

NN = (((1,), (0,)), ((), ()))
NT = (((1,), (1,)), ((), ()))
TN = (((0,), (0,)), ((), ()))


def dot(a, b, dims=NN):
    return lax.dot_general(a, b, dims, preferred_element_type=f32)


def held(*arrays):
    return [pltpu.with_memory_space_constraint(a, pltpu.HBM) for a in arrays]


def params(mib):
    return pltpu.CompilerParams(vmem_limit_bytes=mib << 20)


def send_kernel(x_ref, anchor_ref, face_ref, normed_ref, rows_a_ref, rows_lo_ref, rows_hi_ref):
    x = x_ref[...].astype(f32)
    inverse = lax.rsqrt(jnp.mean(x * x, axis=-1, keepdims=True) + EPSILON)
    normed = (x * inverse).astype(bf16)
    normed_ref[...] = normed

    def picked(index_row):
        cells = lax.broadcasted_iota(jnp.int32, (CELLS, index_row.shape[1]), 0)
        one_hot = (cells == index_row).astype(bf16)
        return dot(one_hot, normed, TN).astype(bf16)

    anchor_rows = picked(anchor_ref[...])
    for slot in range(SLOTS):
        rows_a_ref[slot] = anchor_rows
    rows_lo_ref[...] = picked(face_ref[0:1, :])
    rows_hi_ref[...] = picked(face_ref[1:2, :])


def send_call(x, anchor_row, face_rows):
    return pl.pallas_call(
        send_kernel,
        out_shape=[
            pltpu.HBM((CELLS, D), bf16),
            pltpu.HBM((SLOTS, 32, D), bf16),
            jax.ShapeDtypeStruct((BS, D), bf16),
            jax.ShapeDtypeStruct((BS, D), bf16),
        ],
        compiler_params=params(8),
    )(*held(x, anchor_row, face_rows))


def project_kernel(n_ref, dy_ref, wq_ref, wk_ref, wv_ref, wo_ref, q_ref, k_ref, v_ref, g_ref):
    normed = n_ref[...]
    q_ref[...] = (dot(normed, wq_ref[...]).astype(bf16) * SCALE).astype(bf16)
    k_ref[...] = dot(normed, wk_ref[...]).astype(bf16)
    v_ref[...] = dot(normed, wv_ref[...]).astype(bf16)
    g_ref[...] = dot(dy_ref[...], wo_ref[...], NT).astype(bf16)


def project_call(normed, dy, wq, wk, wv, wo):
    return pl.pallas_call(
        project_kernel,
        out_shape=[jax.ShapeDtypeStruct((CELLS, D), bf16)] * 4,
        compiler_params=params(14),
    )(*held(normed, dy, wq, wk, wv, wo))


def attend_first_kernel(near_ref, count_ref, side_ref, q_ref, k_ref, v_ref, g_ref, n_ref, lo_ref,
                        hi_ref, an_ref, dy_ref, wk_ref, wv_ref, out_ref, rest_ref, keys, values,
                        keys_t, values_t, bias, outside):
    outside[0:BS, :] = lo_ref[...]
    outside[BS:2 * BS, :] = hi_ref[...]
    for slot in range(SLOTS):
        outside[2 * BS + 32 * slot:2 * BS + 32 * slot + 32, :] = an_ref[slot]
    out_ref[1024:1024 + KEY_ROWS, :CELLS] = n_ref[...].T
    out_ref[1024:1024 + KEY_ROWS, CELLS:] = outside[...].T
    out_ref[1024 + KEY_ROWS:, :] = dy_ref[...]
    side = side_ref[0]
    mine = pl.ds(pl.multiple_of(side * SIDE, SIDE), SIDE)
    rest = pl.ds(pl.multiple_of((1 - side) * SIDE, SIDE), SIDE)
    keys[0:CELLS, :] = k_ref[:, mine]
    values[0:CELLS, :] = v_ref[:, mine]
    keys[CELLS:, :] = dot(outside[...], wk_ref[:, mine]).astype(bf16)
    values[CELLS:, :] = dot(outside[...], wv_ref[:, mine]).astype(bf16)
    rest_ref[:, :SIDE] = dot(outside[...], wk_ref[:, rest]).astype(bf16)
    rest_ref[:, SIDE:] = dot(outside[...], wv_ref[:, rest]).astype(bf16)
    attend(near_ref, count_ref, side, q_ref, g_ref, out_ref, keys, values, keys_t, values_t, bias)


def attend_second_kernel(near_ref, count_ref, side_ref, q_ref, k_ref, v_ref, g_ref, rest_ref,
                         out_ref, keys, values, keys_t, values_t, bias):
    side = side_ref[0]
    mine = pl.ds(pl.multiple_of(side * SIDE, SIDE), SIDE)
    keys[0:CELLS, :] = k_ref[:, mine]
    values[0:CELLS, :] = v_ref[:, mine]
    keys[CELLS:, :] = rest_ref[:, :SIDE]
    values[CELLS:, :] = rest_ref[:, SIDE:]
    attend(near_ref, count_ref, side, q_ref, g_ref, out_ref, keys, values, keys_t, values_t, bias)


def attend(near_ref, count_ref, side, q_ref, g_ref, out_ref, keys, values, keys_t, values_t, bias):
    first = pl.multiple_of(side * SIDE, SIDE)
    keys_t[...] = keys[...].T
    values_t[...] = values[...].T

    row = lax.broadcasted_iota(jnp.int32, (BS, BS), 0)
    for block in range(4):
        for j in range(2):
            used = (near_ref[j, 0] == block) | (near_ref[j, 1] == block) | (near_ref[j, 2] == block)
            live = jnp.where(used, BS if block < 2 else count_ref[max(block - 2, 0)], 0)
            bias[block * BS:(block + 1) * BS, j * BS:(j + 1) * BS] = jnp.where(row < live, 0.0, MASKED)

    lane = lax.broadcasted_iota(jnp.int32, (CELLS, PAIR), 1)

    def softmax(scores):
        highest = jnp.max(scores, axis=0, keepdims=True)
        powers = jnp.exp(scores - highest)
        return powers * (1.0 / jnp.sum(powers, axis=0, keepdims=True))

    def score_grad(probs, prob_grad):
        weighted = probs * prob_grad
        return weighted - probs * jnp.sum(weighted, axis=0, keepdims=True)

    for pair in range(PAIRS):
        cols = slice(pair * PAIR, (pair + 1) * PAIR)
        k_pair = keys[:, cols]
        v_pair = values[:, cols]
        from_cols = pl.ds(pl.multiple_of(first + pair * PAIR, PAIR), PAIR)
        q_pair = q_ref[:, from_cols]
        g_pair = g_ref[:, from_cols]
        key_term = None
        value_term = None
        out_t = []
        qg_t = []
        for half in range(2):
            chosen = (lane >= HEAD) if half else (lane < HEAD)
            q_head = jnp.where(chosen, q_pair, jnp.zeros_like(q_pair))
            g_head = jnp.where(chosen, g_pair, jnp.zeros_like(g_pair))
            scores = dot(k_pair, q_head, NT)
            prob_grad = dot(v_pair, g_head, NT)
            near = softmax(scores[:POOL_ROWS] + bias[...])
            anchor = softmax(scores[POOL_ROWS:])
            probs = jnp.concatenate([near.astype(bf16), anchor.astype(bf16)], 0)
            grads = jnp.concatenate(
                [
                    score_grad(near, prob_grad[:POOL_ROWS]).astype(bf16),
                    score_grad(anchor, prob_grad[POOL_ROWS:]).astype(bf16),
                ],
                0,
            )
            head_rows = slice(pair * PAIR + half * HEAD, pair * PAIR + (half + 1) * HEAD)
            out_t.append(dot(values_t[head_rows, :], probs))
            qg_t.append(dot(keys_t[head_rows, :], grads) * SCALE)
            k_new = dot(grads, q_head)
            v_new = dot(probs, g_head)
            key_term = k_new if key_term is None else key_term + k_new
            value_term = v_new if value_term is None else value_term + v_new
        shifted_cols = slice(SIDE + pair * PAIR, SIDE + (pair + 1) * PAIR)
        out_ref[CELLS:CELLS + KEY_ROWS, cols] = key_term.astype(bf16)
        out_ref[CELLS:CELLS + KEY_ROWS, shifted_cols] = value_term.astype(bf16)
        out_ref[0:CELLS, cols] = jnp.concatenate(out_t, 0).astype(bf16).T
        out_ref[0:CELLS, shifted_cols] = jnp.concatenate(qg_t, 0).astype(bf16).T


def attend_scratch(extra):
    return [
        pltpu.VMEM((KEY_ROWS, SIDE), bf16),
        pltpu.VMEM((KEY_ROWS, SIDE), bf16),
        pltpu.VMEM((SIDE, KEY_ROWS), bf16),
        pltpu.VMEM((SIDE, KEY_ROWS), bf16),
        pltpu.VMEM((POOL_ROWS, CELLS), f32),
    ] + [pltpu.VMEM((POOL_ROWS, D), bf16)] * extra


def attend_first_call(near, count, side, queries, received, dy, wk, wv):
    smem = pl.BlockSpec(memory_space=pltpu.SMEM)
    vmem = pl.BlockSpec(memory_space=pltpu.VMEM)
    return pl.pallas_call(
        attend_first_kernel,
        in_specs=[smem] * 3 + [vmem] * 11,
        out_shape=[jax.ShapeDtypeStruct((2048, D), bf16), pltpu.HBM((POOL_ROWS, D), bf16)],
        scratch_shapes=attend_scratch(1),
        compiler_params=params(24),
    )(near, count, side, *queries[:4], *held(queries[4]), *received, *held(dy, wk, wv))


def attend_second_call(near, count, side, queries, rest):
    smem = pl.BlockSpec(memory_space=pltpu.SMEM)
    vmem = pl.BlockSpec(memory_space=pltpu.VMEM)
    return pl.pallas_call(
        attend_second_kernel,
        in_specs=[smem] * 3 + [vmem] * 5,
        out_shape=jax.ShapeDtypeStruct((1024, D), bf16),
        scratch_shapes=attend_scratch(0),
        compiler_params=params(24),
    )(near, count, side, *queries, *held(rest))


def outer_kernel(first_ref, own_ref, got_ref, parts):
    mine = slice(1024, 1024 + KEY_ROWS)

    def block(term, low, cols):
        rows = [term[m + 24 * low:m + 24 * low + 24, cols] for m in range(0, term.shape[0], 48)]
        return jnp.concatenate(rows, 0).astype(bf16)

    def keep(matrix, term, cols):
        for high in range(2):
            for low in range(2):
                parts[4 * matrix + 2 * high + low] = block(term[high * SIDE:(high + 1) * SIDE], low, cols)

    left, right = slice(0, SIDE), slice(SIDE, D)
    keep(0, dot(first_ref[mine, :CELLS], own_ref[0:CELLS, right])
         + dot(got_ref[mine, :CELLS], got_ref[0:CELLS, right]), slice(None))
    pairs = (
        dot(first_ref[mine, :], own_ref[CELLS:1024, :])
        + dot(got_ref[mine, :], got_ref[CELLS:1024, :])
    )
    keep(1, pairs, left)
    keep(2, pairs, right)
    out_term = dot(own_ref[0:CELLS, left], first_ref[1024 + KEY_ROWS:, :], TN) + dot(
        got_ref[0:CELLS, left], got_ref[1024 + KEY_ROWS:, :], TN
    )
    for high in range(2):
        for low in range(2):
            parts[12 + 2 * high + low] = block(out_term, low, right if high else left)


def outer_call(first, own, got):
    return pl.pallas_call(
        outer_kernel,
        out_shape=pltpu.HBM((16, 192, SIDE), bf16),
        compiler_params=params(32),
    )(first, own, got)


def plane_kernel(got_ref, out_ref):
    result = total([got_ref[index] for index in range(16)])
    for z in range(8):
        out_ref[z] = result[24 * z:24 * z + 24].astype(bf16)


def plane_call(got):
    return pl.pallas_call(
        plane_kernel,
        out_shape=jax.ShapeDtypeStruct((8, 24, SIDE), bf16),
        compiler_params=params(10),
    )(got)


def total(rows):
    result = rows[0].astype(f32)
    for row in rows[1:]:
        result = result + row.astype(f32)
    return result


def back_kernel(place_ref, x_ref, first_ref, own_ref, wq_ref, wk_ref, wv_ref, wo_ref,
                mixed_ref, ng_ref, lo_ref, hi_ref, a0_ref, a1_ref, a2_ref, a3_ref, rows):
    core = place_ref[2]
    kv = None
    extra = None
    out = x_ref[...].astype(f32)
    for source, side in ((own_ref, core), (first_ref, 1 - core)):
        half = pl.ds(pl.multiple_of(side * SIDE, SIDE), SIDE)
        term = dot(source[CELLS:1024, :SIDE], wk_ref[:, half], NT)
        kv = term if kv is None else kv + term
        kv = kv + dot(source[CELLS:1024, SIDE:], wv_ref[:, half], NT)
        term = dot(source[0:CELLS, SIDE:], wq_ref[:, half], NT)
        extra = term if extra is None else extra + term
        out = out + dot(source[0:CELLS, :SIDE], wo_ref[half, :])
    ng_ref[...] = kv[:CELLS] + extra
    lo_ref[...] = kv[CELLS:CELLS + BS].astype(bf16)
    hi_ref[...] = kv[CELLS + BS:POOL_ROWS].astype(bf16)
    for y in range(4):
        rows[y] = kv[POOL_ROWS + 64 * y:POOL_ROWS + 64 * y + 64].astype(bf16)
    for step, target in enumerate((a0_ref, a1_ref, a2_ref, a3_ref)):
        target[...] = rows[(place_ref[1] + step) % 4]
    mixed_ref[...] = out.astype(bf16)


def back_call(place, x, first, own, wq, wk, wv, wo):
    smem = pl.BlockSpec(memory_space=pltpu.SMEM)
    vmem = pl.BlockSpec(memory_space=pltpu.VMEM)
    return pl.pallas_call(
        back_kernel,
        in_specs=[smem] + [vmem] * 7,
        out_shape=[
            jax.ShapeDtypeStruct((CELLS, D), bf16),
            pltpu.HBM((CELLS, D), f32),
            jax.ShapeDtypeStruct((BS, D), bf16),
            jax.ShapeDtypeStruct((BS, D), bf16),
        ] + [jax.ShapeDtypeStruct((64, D), bf16)] * 4,
        scratch_shapes=[pltpu.VMEM((4, 64, D), bf16)],
        compiler_params=params(24),
    )(place, *held(x, first, own, wq, wk, wv, wo))


def share_kernel(place_ref, s0, s1, s2, s3, keep_ref, send_ref, rows):
    summed = total([ref[...] for ref in (s0, s1, s2, s3)])
    rows[0] = summed[:32]
    rows[1] = summed[32:]
    xh = place_ref[0] // 2
    keep_ref[...] = rows[xh]
    send_ref[...] = rows[1 - xh].astype(bf16)


def share_call(place, shares):
    smem = pl.BlockSpec(memory_space=pltpu.SMEM)
    vmem = pl.BlockSpec(memory_space=pltpu.VMEM)
    return pl.pallas_call(
        share_kernel,
        in_specs=[smem] + [vmem] * 4,
        out_shape=[pltpu.HBM((32, D), f32), jax.ShapeDtypeStruct((32, D), bf16)],
        scratch_shapes=[pltpu.VMEM((2, 32, D), f32)],
        compiler_params=params(4),
    )(place, *shares)


def final_kernel(x_ref, dy_ref, own_ref, lo_ref, hi_ref, anchor_ref, face_ref, kept_ref, crossed_ref,
                 out_ref):
    x = x_ref[...].astype(f32)
    inverse = lax.rsqrt(jnp.mean(x * x, axis=-1, keepdims=True) + EPSILON)

    def placed(index_row, rows):
        cells = lax.broadcasted_iota(jnp.int32, (CELLS, index_row.shape[1]), 0)
        return dot((cells == index_row).astype(bf16), rows)

    shares = kept_ref[...] + crossed_ref[...].astype(f32)
    high = shares.astype(bf16)
    low = (shares - high.astype(f32)).astype(bf16)
    normed_grad = (
        own_ref[...]
        + placed(face_ref[0:1, :], lo_ref[...])
        + placed(face_ref[1:2, :], hi_ref[...])
        + placed(anchor_ref[...], high)
        + placed(anchor_ref[...], low)
    )
    cube = inverse * inverse * inverse
    out_ref[...] = (
        dy_ref[...].astype(f32)
        + inverse * normed_grad
        - x * cube * jnp.mean(normed_grad * x, axis=-1, keepdims=True)
    ).astype(bf16)


def final_call(x, dy, own, from_lo, from_hi, anchor_row, face_rows, kept, crossed):
    return pl.pallas_call(
        final_kernel,
        out_shape=jax.ShapeDtypeStruct((CELLS, D), bf16),
        compiler_params=params(12),
    )(*held(x, dy, own), from_lo, from_hi, *held(anchor_row, face_rows, kept), crossed)


def swapped(value, axis):
    return lax.ppermute(value, axis, [(0, 1), (1, 0)])


def spread(arrays, axis):
    return [arrays[0]] + [
        lax.ppermute(arrays[k], axis, [(i, (i + k) % 4) for i in range(4)]) for k in (1, 2, 3)
    ]


def along(value, step):
    count = 32
    pairs = [(i, i + step) for i in range(count) if 0 <= i + step < count]
    return lax.ppermute(value, ("z", "xl", "core"), pairs)


X_RING = ("xh", "xl")
SLOT = ("y", "xh")


def settle_kernel(place_ref, rows_ref, own_ref, other_ref):
    rows = total([rows_ref[index] for index in range(8)])
    upper = jnp.where(place_ref[1] == 3, place_ref[0] // 2, place_ref[2]) == 1
    own_ref[...] = jnp.where(upper, rows[12:], rows[:12])
    other_ref[...] = jnp.where(upper, rows[:12], rows[12:])


def settle_call(place, rows):
    smem = pl.BlockSpec(memory_space=pltpu.SMEM)
    vmem = pl.BlockSpec(memory_space=pltpu.VMEM)
    return pl.pallas_call(
        settle_kernel,
        in_specs=[smem, vmem],
        out_shape=[jax.ShapeDtypeStruct((12, SIDE), f32)] * 2,
        compiler_params=params(4),
    )(place, rows)


def settled(place, rows):
    own, other = settle_call(place, rows)
    last = place[1] == 3
    core = place[2]

    def device(y_at, xh_at, core_at):
        return (y_at * 2 + xh_at) * 2 + core_at

    turn, swap = [], []
    for h in range(2):
        for r in range(2):
            turn.append((device(3, h, r), device(3, r, h)))
            swap.append((device(3, h, r), device(3, r, 1 - h)))
            swap += [(device(m, h, r), device(m, h, 1 - r)) for m in range(3)]
    axes = ("y", "xh", "core")
    turned = lax.ppermute(own, axes, turn)
    here = jnp.where(last, turned, own)
    there = lax.ppermute(other, axes, swap)
    return jnp.where(
        core == 0, jnp.concatenate([here, there], 1), jnp.concatenate([there, here], 1)
    )


def body(
    cell_features,
    cotangent,
    query_weight,
    key_weight,
    value_weight,
    out_weight,
    anchor_index,
    face_cells,
    halo_count,
    neighbour_blocks,
):
    x = cell_features[0]
    dy = cotangent[0]
    face_rows = face_cells.reshape(2, BS)
    near = neighbour_blocks.reshape(2, NB)
    count = halo_count.reshape(2)
    weights = (query_weight, key_weight, value_weight, out_weight)
    core = lax.axis_index("core").astype(jnp.int32).reshape(1)
    place = jnp.stack(
        [2 * lax.axis_index("xh") + lax.axis_index("xl"), lax.axis_index("y"), core[0]]
    ).astype(jnp.int32)

    normed, sent_anchors, sent_lo, sent_hi = send_call(x, anchor_index, face_rows)
    from_lo = along(sent_hi, 1)
    from_hi = along(sent_lo, -1)
    anchors = lax.all_to_all(sent_anchors, SLOT, 0, 0, tiled=True)
    q, k, v, g = project_call(normed, dy, *weights)

    first, rest = attend_first_call(
        near, count, 1 - core, (q, k, v, g, normed), (from_lo, from_hi, anchors), dy,
        key_weight, value_weight,
    )
    got = swapped(first, "core")
    own = attend_second_call(near, count, core, (q, k, v, g), rest)

    parts = outer_call(first, own, got)
    own, parts = lax.optimization_barrier((own, parts))
    plane = lax.all_to_all(parts, ("y", "xh", "xl"), 0, 0, tiled=True)
    mixed, own_grad, to_lo, to_hi, *shares = back_call(place, x, first, own, *weights)
    back_hi = along(to_lo, -1)
    back_lo = along(to_hi, 1)
    kept, crossing = share_call(place, spread(shares, "y"))
    plane, kept, crossing, back_hi, back_lo = lax.optimization_barrier(
        (plane, kept, crossing, back_hi, back_lo)
    )
    crossed = swapped(crossing, "xh")
    column = plane_call(plane)
    column = lax.all_to_all(column, "z", 0, 0, tiled=True)
    column, own_grad = lax.optimization_barrier((column, own_grad))
    cell_grad = final_call(
        x, dy, own_grad, back_lo, back_hi, anchor_index, face_rows, kept, crossed
    )
    weight_grads = settled(place, column)
    return mixed[None], cell_grad[None], weight_grads


def solution(mesh):
    fine = Mesh(mesh.devices.reshape(4, 2, 8, 2, 2), ("y", "xh", "z", "xl", "core"))
    dom = ("z", "xl", "core")
    blk = ("y", "xh")
    return jax.shard_map(
        body,
        mesh=fine,
        in_specs=(
            P(dom, blk, None),
            P(dom, blk, None),
            P(),
            P(),
            P(),
            P(),
            P(dom, blk),
            P(dom, blk, None, None),
            P(dom, blk, None),
            P(dom, blk, None),
        ),
        out_specs=(P(dom, blk, None), P(dom, blk, None), P(blk + dom, None)),
        check_vma=False,
    )
```

```python
import functools

import jax
import jax.numpy as jnp
from jax import lax
from jax.experimental import pallas as pl
from jax.experimental.pallas import tpu as pltpu
from jax.sharding import Mesh, PartitionSpec as P

HEADS = 12
BS = 128
NB = 3
D = 768
CELLS = 256
ANCHORS = 256
POOL_ROWS = 512
KEY_ROWS = 768
HEAD = 64
SIDE = 384
PAIRS = 3
SLOTS = 8
PAIR = 128
SCALE = 0.125
EPSILON = 1e-06
MASKED = -1e30

f32 = jnp.float32
bf16 = jnp.bfloat16

NN = (((1,), (0,)), ((), ()))
NT = (((1,), (1,)), ((), ()))
TN = (((0,), (0,)), ((), ()))


def dot(a, b, dims=NN):
    return lax.dot_general(a, b, dims, preferred_element_type=f32)


def held(*arrays):
    return [pltpu.with_memory_space_constraint(a, pltpu.HBM) for a in arrays]


def params(mib):
    return pltpu.CompilerParams(vmem_limit_bytes=mib << 20)


def send_kernel(x_ref, anchor_ref, face_ref, normed_ref, rows_a_ref, rows_lo_ref, rows_hi_ref):
    x = x_ref[...].astype(f32)
    inverse = lax.rsqrt(jnp.mean(x * x, axis=-1, keepdims=True) + EPSILON)
    normed = (x * inverse).astype(bf16)
    normed_ref[...] = normed

    def picked(index_row):
        cells = lax.broadcasted_iota(jnp.int32, (CELLS, index_row.shape[1]), 0)
        one_hot = (cells == index_row).astype(bf16)
        return dot(one_hot, normed, TN).astype(bf16)

    anchor_rows = picked(anchor_ref[...])
    for slot in range(SLOTS):
        rows_a_ref[slot] = anchor_rows
    rows_lo_ref[...] = picked(face_ref[0:1, :])
    rows_hi_ref[...] = picked(face_ref[1:2, :])


def send_call(x, anchor_row, face_rows):
    return pl.pallas_call(
        send_kernel,
        out_shape=[
            pltpu.HBM((CELLS, D), bf16),
            pltpu.HBM((SLOTS, 32, D), bf16),
            jax.ShapeDtypeStruct((BS, D), bf16),
            jax.ShapeDtypeStruct((BS, D), bf16),
        ],
        compiler_params=params(8),
    )(*held(x, anchor_row, face_rows))


def project_kernel(n_ref, dy_ref, wq_ref, wk_ref, wv_ref, wo_ref, q_ref, k_ref, v_ref, g_ref):
    normed = n_ref[...]
    q_ref[...] = (dot(normed, wq_ref[...]).astype(bf16) * SCALE).astype(bf16)
    k_ref[...] = dot(normed, wk_ref[...]).astype(bf16)
    v_ref[...] = dot(normed, wv_ref[...]).astype(bf16)
    g_ref[...] = dot(dy_ref[...], wo_ref[...], NT).astype(bf16)


def project_call(normed, dy, wq, wk, wv, wo):
    return pl.pallas_call(
        project_kernel,
        out_shape=[jax.ShapeDtypeStruct((CELLS, D), bf16)] * 4,
        compiler_params=params(14),
    )(*held(normed, dy, wq, wk, wv, wo))


def attend_first_kernel(near_ref, count_ref, side_ref, q_ref, k_ref, v_ref, g_ref, n_ref, lo_ref,
                        hi_ref, an_ref, dy_ref, wk_ref, wv_ref, out_ref, rest_ref, keys, values,
                        keys_t, values_t, bias, outside):
    outside[0:BS, :] = lo_ref[...]
    outside[BS:2 * BS, :] = hi_ref[...]
    for slot in range(SLOTS):
        outside[2 * BS + 32 * slot:2 * BS + 32 * slot + 32, :] = an_ref[slot]
    out_ref[1024:1024 + KEY_ROWS, :CELLS] = n_ref[...].T
    out_ref[1024:1024 + KEY_ROWS, CELLS:] = outside[...].T
    out_ref[1024 + KEY_ROWS:, :] = dy_ref[...]
    side = side_ref[0]
    mine = pl.ds(pl.multiple_of(side * SIDE, SIDE), SIDE)
    rest = pl.ds(pl.multiple_of((1 - side) * SIDE, SIDE), SIDE)
    keys[0:CELLS, :] = k_ref[:, mine]
    values[0:CELLS, :] = v_ref[:, mine]
    keys[CELLS:, :] = dot(outside[...], wk_ref[:, mine]).astype(bf16)
    values[CELLS:, :] = dot(outside[...], wv_ref[:, mine]).astype(bf16)
    rest_ref[:, :SIDE] = dot(outside[...], wk_ref[:, rest]).astype(bf16)
    rest_ref[:, SIDE:] = dot(outside[...], wv_ref[:, rest]).astype(bf16)
    attend(near_ref, count_ref, side, q_ref, g_ref, out_ref, keys, values, keys_t, values_t, bias)


def attend_second_kernel(near_ref, count_ref, side_ref, q_ref, k_ref, v_ref, g_ref, rest_ref,
                         out_ref, keys, values, keys_t, values_t, bias):
    side = side_ref[0]
    mine = pl.ds(pl.multiple_of(side * SIDE, SIDE), SIDE)
    keys[0:CELLS, :] = k_ref[:, mine]
    values[0:CELLS, :] = v_ref[:, mine]
    keys[CELLS:, :] = rest_ref[:, :SIDE]
    values[CELLS:, :] = rest_ref[:, SIDE:]
    attend(near_ref, count_ref, side, q_ref, g_ref, out_ref, keys, values, keys_t, values_t, bias)


def attend(near_ref, count_ref, side, q_ref, g_ref, out_ref, keys, values, keys_t, values_t, bias):
    first = pl.multiple_of(side * SIDE, SIDE)
    keys_t[...] = keys[...].T
    values_t[...] = values[...].T

    row = lax.broadcasted_iota(jnp.int32, (BS, BS), 0)
    for block in range(4):
        for j in range(2):
            used = (near_ref[j, 0] == block) | (near_ref[j, 1] == block) | (near_ref[j, 2] == block)
            live = jnp.where(used, BS if block < 2 else count_ref[max(block - 2, 0)], 0)
            bias[block * BS:(block + 1) * BS, j * BS:(j + 1) * BS] = jnp.where(row < live, 0.0, MASKED)

    lane = lax.broadcasted_iota(jnp.int32, (CELLS, PAIR), 1)

    def softmax(scores):
        highest = jnp.max(scores, axis=0, keepdims=True)
        powers = jnp.exp(scores - highest)
        return powers * (1.0 / jnp.sum(powers, axis=0, keepdims=True))

    def score_grad(probs, prob_grad):
        weighted = probs * prob_grad
        return weighted - probs * jnp.sum(weighted, axis=0, keepdims=True)

    for pair in range(PAIRS):
        cols = slice(pair * PAIR, (pair + 1) * PAIR)
        k_pair = keys[:, cols]
        v_pair = values[:, cols]
        from_cols = pl.ds(pl.multiple_of(first + pair * PAIR, PAIR), PAIR)
        q_pair = q_ref[:, from_cols]
        g_pair = g_ref[:, from_cols]
        key_term = None
        value_term = None
        out_t = []
        qg_t = []
        for half in range(2):
            chosen = (lane >= HEAD) if half else (lane < HEAD)
            q_head = jnp.where(chosen, q_pair, jnp.zeros_like(q_pair))
            g_head = jnp.where(chosen, g_pair, jnp.zeros_like(g_pair))
            scores = dot(k_pair, q_head, NT)
            prob_grad = dot(v_pair, g_head, NT)
            near = softmax(scores[:POOL_ROWS] + bias[...])
            anchor = softmax(scores[POOL_ROWS:])
            probs = jnp.concatenate([near.astype(bf16), anchor.astype(bf16)], 0)
            grads = jnp.concatenate(
                [
                    score_grad(near, prob_grad[:POOL_ROWS]).astype(bf16),
                    score_grad(anchor, prob_grad[POOL_ROWS:]).astype(bf16),
                ],
                0,
            )
            head_rows = slice(pair * PAIR + half * HEAD, pair * PAIR + (half + 1) * HEAD)
            out_t.append(dot(values_t[head_rows, :], probs))
            qg_t.append(dot(keys_t[head_rows, :], grads) * SCALE)
            k_new = dot(grads, q_head)
            v_new = dot(probs, g_head)
            key_term = k_new if key_term is None else key_term + k_new
            value_term = v_new if value_term is None else value_term + v_new
        shifted_cols = slice(SIDE + pair * PAIR, SIDE + (pair + 1) * PAIR)
        out_ref[CELLS:CELLS + KEY_ROWS, cols] = key_term.astype(bf16)
        out_ref[CELLS:CELLS + KEY_ROWS, shifted_cols] = value_term.astype(bf16)
        out_ref[0:CELLS, cols] = jnp.concatenate(out_t, 0).astype(bf16).T
        out_ref[0:CELLS, shifted_cols] = jnp.concatenate(qg_t, 0).astype(bf16).T


def attend_scratch(extra):
    return [
        pltpu.VMEM((KEY_ROWS, SIDE), bf16),
        pltpu.VMEM((KEY_ROWS, SIDE), bf16),
        pltpu.VMEM((SIDE, KEY_ROWS), bf16),
        pltpu.VMEM((SIDE, KEY_ROWS), bf16),
        pltpu.VMEM((POOL_ROWS, CELLS), f32),
    ] + [pltpu.VMEM((POOL_ROWS, D), bf16)] * extra


def attend_first_call(near, count, side, queries, received, dy, wk, wv):
    smem = pl.BlockSpec(memory_space=pltpu.SMEM)
    vmem = pl.BlockSpec(memory_space=pltpu.VMEM)
    return pl.pallas_call(
        attend_first_kernel,
        in_specs=[smem] * 3 + [vmem] * 11,
        out_shape=[jax.ShapeDtypeStruct((2048, D), bf16), pltpu.HBM((POOL_ROWS, D), bf16)],
        scratch_shapes=attend_scratch(1),
        compiler_params=params(24),
    )(near, count, side, *queries[:4], *held(queries[4]), *received, *held(dy, wk, wv))


def attend_second_call(near, count, side, queries, rest):
    smem = pl.BlockSpec(memory_space=pltpu.SMEM)
    vmem = pl.BlockSpec(memory_space=pltpu.VMEM)
    return pl.pallas_call(
        attend_second_kernel,
        in_specs=[smem] * 3 + [vmem] * 5,
        out_shape=jax.ShapeDtypeStruct((1024, D), bf16),
        scratch_shapes=attend_scratch(0),
        compiler_params=params(24),
    )(near, count, side, *queries, *held(rest))


def outer_kernel(first_ref, own_ref, got_ref, parts):
    mine = slice(1024, 1024 + KEY_ROWS)

    def block(term, low, cols):
        starts = [48 * z + 24 * low for odd in range(2) for z in range(odd, 8, 2)]
        return jnp.concatenate([term[m:m + 24, cols] for m in starts], 0).astype(bf16)

    def keep(matrix, term, cols):
        for high in range(2):
            for low in range(2):
                parts[4 * matrix + 2 * high + low] = block(term[high * SIDE:(high + 1) * SIDE], low, cols)

    left, right = slice(0, SIDE), slice(SIDE, D)
    keep(0, dot(first_ref[mine, :CELLS], own_ref[0:CELLS, right])
         + dot(got_ref[mine, :CELLS], got_ref[0:CELLS, right]), slice(None))
    pairs = (
        dot(first_ref[mine, :], own_ref[CELLS:1024, :])
        + dot(got_ref[mine, :], got_ref[CELLS:1024, :])
    )
    keep(1, pairs, left)
    keep(2, pairs, right)
    out_term = dot(own_ref[0:CELLS, left], first_ref[1024 + KEY_ROWS:, :], TN) + dot(
        got_ref[0:CELLS, left], got_ref[1024 + KEY_ROWS:, :], TN
    )
    for high in range(2):
        for low in range(2):
            parts[12 + 2 * high + low] = block(out_term, low, right if high else left)


def outer_call(first, own, got):
    return pl.pallas_call(
        outer_kernel,
        out_shape=pltpu.HBM((16, 192, SIDE), bf16),
        compiler_params=params(32),
    )(first, own, got)


def plane_kernel(got_ref, out_ref):
    result = total([got_ref[index] for index in range(32)])
    for z in range(4):
        out_ref[z] = result[24 * z:24 * z + 24].astype(bf16)


def plane_call(got):
    return pl.pallas_call(
        plane_kernel,
        out_shape=jax.ShapeDtypeStruct((4, 24, SIDE), bf16),
        compiler_params=params(10),
    )(got)


def total(rows):
    result = rows[0].astype(f32)
    for row in rows[1:]:
        result = result + row.astype(f32)
    return result


def started(pairs, sems):
    copies = [pltpu.make_async_copy(src, dst, sems.at[i]) for i, (src, dst) in enumerate(pairs)]
    for copy in copies:
        copy.start()
    return copies


def waited(copies):
    for copy in copies:
        copy.wait()


def halves(core):
    return [pl.ds(pl.multiple_of(side * SIDE, SIDE), SIDE) for side in (core, 1 - core)]


def back_kernel(place_ref, x_ref, first_any, own_any, wq_any, wk_any, wv_any, wo_any, mixed_ref,
                ng_ref, lo_ref, hi_ref, a0_ref, a1_ref, a2_ref, a3_ref, rows, own_ref, first_ref,
                wq_ref, wk_ref, wv_ref, wo_ref, sems):
    loads = started(
        [
            (wk_any, wk_ref), (own_any, own_ref), (wv_any, wv_ref),
            (first_any.at[0:1024, :], first_ref), (wq_any, wq_ref), (wo_any, wo_ref),
        ],
        sems,
    )
    sources = list(zip((own_ref, first_ref), halves(place_ref[2])))
    waited(loads[:2])
    kv = dot(own_ref[CELLS:, :SIDE], wk_ref[:, sources[0][1]], NT)
    waited(loads[2:3])
    kv = kv + dot(own_ref[CELLS:, SIDE:], wv_ref[:, sources[0][1]], NT)
    waited(loads[3:])
    kv = kv + dot(first_ref[CELLS:, :SIDE], wk_ref[:, sources[1][1]], NT)
    kv = kv + dot(first_ref[CELLS:, SIDE:], wv_ref[:, sources[1][1]], NT)
    lo_ref[...] = kv[CELLS:CELLS + BS].astype(bf16)
    hi_ref[...] = kv[CELLS + BS:POOL_ROWS].astype(bf16)
    for y in range(4):
        rows[y] = kv[POOL_ROWS + 64 * y:POOL_ROWS + 64 * y + 64].astype(bf16)
    for step, target in enumerate((a0_ref, a1_ref, a2_ref, a3_ref)):
        target[...] = rows[(place_ref[1] + step) % 4]
    grad = kv[:CELLS]
    out = x_ref[...].astype(f32)
    for source, half in sources:
        grad = grad + dot(source[:CELLS, SIDE:], wq_ref[:, half], NT)
        out = out + dot(source[:CELLS, :SIDE], wo_ref[half, :])
    ng_ref[...] = grad
    mixed_ref[...] = out.astype(bf16)


def back_call(place, x, first, own, wq, wk, wv, wo):
    smem = pl.BlockSpec(memory_space=pltpu.SMEM)
    whole = pl.BlockSpec(memory_space=pltpu.VMEM)
    anywhere = pl.BlockSpec(memory_space=pl.ANY)
    return pl.pallas_call(
        back_kernel,
        in_specs=[smem, whole] + [anywhere] * 6,
        out_shape=[jax.ShapeDtypeStruct((CELLS, D), bf16), pltpu.HBM((CELLS, D), f32)]
        + [jax.ShapeDtypeStruct((BS, D), bf16)] * 2
        + [jax.ShapeDtypeStruct((64, D), bf16)] * 4,
        scratch_shapes=[pltpu.VMEM((4, 64, D), bf16)]
        + [pltpu.VMEM((1024, D), bf16)] * 2
        + [pltpu.VMEM((D, D), bf16)] * 4
        + [pltpu.SemaphoreType.DMA((6,))],
        compiler_params=params(24),
    )(place, *held(x, first, own, wq, wk, wv, wo))


def share_kernel(place_ref, s0, s1, s2, s3, keep_ref, send_ref, rows):
    summed = total([ref[...] for ref in (s0, s1, s2, s3)])
    rows[0] = summed[:32]
    rows[1] = summed[32:]
    xh = place_ref[0] // 2
    keep_ref[...] = rows[xh]
    send_ref[...] = rows[1 - xh].astype(bf16)


def share_call(place, shares):
    smem = pl.BlockSpec(memory_space=pltpu.SMEM)
    vmem = pl.BlockSpec(memory_space=pltpu.VMEM)
    return pl.pallas_call(
        share_kernel,
        in_specs=[smem] + [vmem] * 4,
        out_shape=[pltpu.HBM((32, D), f32), jax.ShapeDtypeStruct((32, D), bf16)],
        scratch_shapes=[pltpu.VMEM((2, 32, D), f32)],
        compiler_params=params(4),
    )(place, *shares)


def final_kernel(x_ref, dy_ref, own_ref, lo_ref, hi_ref, anchor_ref, face_ref, kept_ref, crossed_ref,
                 out_ref):
    x = x_ref[...].astype(f32)
    inverse = lax.rsqrt(jnp.mean(x * x, axis=-1, keepdims=True) + EPSILON)

    def placed(index_row, rows):
        cells = lax.broadcasted_iota(jnp.int32, (CELLS, index_row.shape[1]), 0)
        return dot((cells == index_row).astype(bf16), rows)

    shares = kept_ref[...] + crossed_ref[...].astype(f32)
    high = shares.astype(bf16)
    low = (shares - high.astype(f32)).astype(bf16)
    normed_grad = (
        own_ref[...]
        + placed(face_ref[0:1, :], lo_ref[...])
        + placed(face_ref[1:2, :], hi_ref[...])
        + placed(anchor_ref[...], high)
        + placed(anchor_ref[...], low)
    )
    cube = inverse * inverse * inverse
    out_ref[...] = (
        dy_ref[...].astype(f32)
        + inverse * normed_grad
        - x * cube * jnp.mean(normed_grad * x, axis=-1, keepdims=True)
    ).astype(bf16)


def final_call(x, dy, own, from_lo, from_hi, anchor_row, face_rows, kept, crossed):
    return pl.pallas_call(
        final_kernel,
        out_shape=jax.ShapeDtypeStruct((CELLS, D), bf16),
        compiler_params=params(12),
    )(*held(x, dy, own), from_lo, from_hi, *held(anchor_row, face_rows, kept), crossed)


def swapped(value, axis):
    return lax.ppermute(value, axis, [(0, 1), (1, 0)])


def spread(arrays, axis):
    return [arrays[0]] + [
        lax.ppermute(arrays[k], axis, [(i, (i + k) % 4) for i in range(4)]) for k in (1, 2, 3)
    ]


def along(value, step):
    count = 32
    pairs = [(i, i + step) for i in range(count) if 0 <= i + step < count]
    return lax.ppermute(value, ("zh", "zl", "xl", "core"), pairs)


X_RING = ("xh", "xl")
SLOT = ("y", "xh")


def settle_kernel(place_ref, rows_ref, own_ref, other_ref):
    rows = total([rows_ref[index] for index in range(4)])
    upper = jnp.where(place_ref[1] == 3, place_ref[0] // 2, place_ref[2]) == 1
    own_ref[...] = jnp.where(upper, rows[12:], rows[:12])
    other_ref[...] = jnp.where(upper, rows[:12], rows[12:])


def settle_call(place, rows):
    smem = pl.BlockSpec(memory_space=pltpu.SMEM)
    vmem = pl.BlockSpec(memory_space=pltpu.VMEM)
    return pl.pallas_call(
        settle_kernel,
        in_specs=[smem, vmem],
        out_shape=[jax.ShapeDtypeStruct((12, SIDE), f32)] * 2,
        compiler_params=params(4),
    )(place, rows)


def settled(place, rows):
    own, other = settle_call(place, rows)
    last = place[1] == 3
    core = place[2]

    def device(y_at, xh_at, core_at):
        return (y_at * 2 + xh_at) * 2 + core_at

    turn, swap = [], []
    for h in range(2):
        for r in range(2):
            turn.append((device(3, h, r), device(3, r, h)))
            swap.append((device(3, h, r), device(3, r, 1 - h)))
            swap += [(device(m, h, r), device(m, h, 1 - r)) for m in range(3)]
    axes = ("y", "xh", "core")
    turned = lax.ppermute(own, axes, turn)
    here = jnp.where(last, turned, own)
    there = lax.ppermute(other, axes, swap)
    return jnp.where(
        core == 0, jnp.concatenate([here, there], 1), jnp.concatenate([there, here], 1)
    )


def body(
    cell_features,
    cotangent,
    query_weight,
    key_weight,
    value_weight,
    out_weight,
    anchor_index,
    face_cells,
    halo_count,
    neighbour_blocks,
):
    x = cell_features[0]
    dy = cotangent[0]
    face_rows = face_cells.reshape(2, BS)
    near = neighbour_blocks.reshape(2, NB)
    count = halo_count.reshape(2)
    weights = (query_weight, key_weight, value_weight, out_weight)
    core = lax.axis_index("core").astype(jnp.int32).reshape(1)
    place = jnp.stack(
        [2 * lax.axis_index("xh") + lax.axis_index("xl"), lax.axis_index("y"), core[0]]
    ).astype(jnp.int32)

    normed, sent_anchors, sent_lo, sent_hi = send_call(x, anchor_index, face_rows)
    from_lo = along(sent_hi, 1)
    from_hi = along(sent_lo, -1)
    anchors = lax.all_to_all(sent_anchors, SLOT, 0, 0, tiled=True)
    q, k, v, g = project_call(normed, dy, *weights)

    first, rest = attend_first_call(
        near, count, 1 - core, (q, k, v, g, normed), (from_lo, from_hi, anchors), dy,
        key_weight, value_weight,
    )
    got = swapped(first, "core")
    own = attend_second_call(near, count, core, (q, k, v, g), rest)

    parts = outer_call(first, own, got)
    own, parts = lax.optimization_barrier((own, parts))
    plane = lax.all_to_all(parts.reshape(32, 96, SIDE), ("y", "xh", "xl", "zl"), 0, 0, tiled=True)
    mixed, own_grad, to_lo, to_hi, *shares = back_call(place, x, first, own, *weights)
    shares = spread(shares, "y")
    back_hi = along(to_lo, -1)
    back_lo = along(to_hi, 1)
    plane, shares[1] = lax.optimization_barrier((plane, shares[1]))
    kept, crossing = share_call(place, shares)
    crossed = swapped(crossing, "xh")
    column = plane_call(plane)
    column, back_hi, back_lo = lax.optimization_barrier((column, back_hi, back_lo))
    column = lax.all_to_all(column, "zh", 0, 0, tiled=True)
    column, own_grad = lax.optimization_barrier((column, own_grad))
    cell_grad = final_call(
        x, dy, own_grad, back_lo, back_hi, anchor_index, face_rows, kept, crossed
    )
    weight_grads = settled(place, column)
    return mixed[None], cell_grad[None], weight_grads


def solution(mesh):
    fine = Mesh(mesh.devices.reshape(4, 2, 4, 2, 2, 2), ("y", "xh", "zh", "zl", "xl", "core"))
    dom = ("zh", "zl", "xl", "core")
    blk = ("y", "xh")
    return jax.shard_map(
        body,
        mesh=fine,
        in_specs=(
            P(dom, blk, None),
            P(dom, blk, None),
            P(),
            P(),
            P(),
            P(),
            P(dom, blk),
            P(dom, blk, None, None),
            P(dom, blk, None),
            P(dom, blk, None),
        ),
        out_specs=(P(dom, blk, None), P(dom, blk, None), P(blk + dom, None)),
        check_vma=False,
    )
```

```python
import functools

import jax
import jax.numpy as jnp
from jax import lax
from jax.experimental import pallas as pl
from jax.experimental.pallas import tpu as pltpu
from jax.sharding import Mesh, PartitionSpec as P

HEADS = 12
BS = 128
NB = 3
D = 768
CELLS = 256
ANCHORS = 256
POOL_ROWS = 512
KEY_ROWS = 768
HEAD = 64
SIDE = 384
PAIRS = 3
SLOTS = 8
PAIR = 128
SCALE = 0.125
EPSILON = 1e-06
MASKED = -1e30

f32 = jnp.float32
bf16 = jnp.bfloat16

NN = (((1,), (0,)), ((), ()))
NT = (((1,), (1,)), ((), ()))
TN = (((0,), (0,)), ((), ()))


def dot(a, b, dims=NN):
    return lax.dot_general(a, b, dims, preferred_element_type=f32)


def held(*arrays):
    return [pltpu.with_memory_space_constraint(a, pltpu.HBM) for a in arrays]


def params(mib):
    return pltpu.CompilerParams(vmem_limit_bytes=mib << 20)


def send_kernel(x_ref, anchor_ref, face_ref, normed_ref, rows_a_ref, rows_lo_ref, rows_hi_ref):
    x = x_ref[...].astype(f32)
    inverse = lax.rsqrt(jnp.mean(x * x, axis=-1, keepdims=True) + EPSILON)
    normed = (x * inverse).astype(bf16)
    normed_ref[...] = normed

    def picked(index_row):
        cells = lax.broadcasted_iota(jnp.int32, (CELLS, index_row.shape[1]), 0)
        one_hot = (cells == index_row).astype(bf16)
        return dot(one_hot, normed, TN).astype(bf16)

    anchor_rows = picked(anchor_ref[...])
    for slot in range(SLOTS):
        rows_a_ref[slot] = anchor_rows
    rows_lo_ref[...] = picked(face_ref[0:1, :])
    rows_hi_ref[...] = picked(face_ref[1:2, :])


def send_call(x, anchor_row, face_rows):
    return pl.pallas_call(
        send_kernel,
        out_shape=[
            pltpu.HBM((CELLS, D), bf16),
            pltpu.HBM((SLOTS, 32, D), bf16),
            jax.ShapeDtypeStruct((BS, D), bf16),
            jax.ShapeDtypeStruct((BS, D), bf16),
        ],
        compiler_params=params(8),
    )(*held(x, anchor_row, face_rows))


def project_kernel(n_ref, dy_ref, wq_ref, wk_ref, wv_ref, wo_ref, q_ref, k_ref, v_ref, g_ref):
    normed = n_ref[...]
    q_ref[...] = (dot(normed, wq_ref[...]).astype(bf16) * SCALE).astype(bf16)
    k_ref[...] = dot(normed, wk_ref[...]).astype(bf16)
    v_ref[...] = dot(normed, wv_ref[...]).astype(bf16)
    g_ref[...] = dot(dy_ref[...], wo_ref[...], NT).astype(bf16)


def project_call(normed, dy, wq, wk, wv, wo):
    return pl.pallas_call(
        project_kernel,
        out_shape=[jax.ShapeDtypeStruct((CELLS, D), bf16)] * 4,
        compiler_params=params(14),
    )(*held(normed, dy, wq, wk, wv, wo))


def attend_first_kernel(near_ref, count_ref, side_ref, q_ref, k_ref, v_ref, g_ref, n_ref, lo_ref,
                        hi_ref, an_ref, dy_ref, wk_ref, wv_ref, out_ref, rest_ref, keys, values,
                        keys_t, values_t, bias, outside):
    outside[0:BS, :] = lo_ref[...]
    outside[BS:2 * BS, :] = hi_ref[...]
    for slot in range(SLOTS):
        outside[2 * BS + 32 * slot:2 * BS + 32 * slot + 32, :] = an_ref[slot]
    out_ref[1024:1024 + KEY_ROWS, :CELLS] = n_ref[...].T
    out_ref[1024:1024 + KEY_ROWS, CELLS:] = outside[...].T
    out_ref[1024 + KEY_ROWS:, :] = dy_ref[...]
    side = side_ref[0]
    mine = pl.ds(pl.multiple_of(side * SIDE, SIDE), SIDE)
    rest = pl.ds(pl.multiple_of((1 - side) * SIDE, SIDE), SIDE)
    keys[0:CELLS, :] = k_ref[:, mine]
    values[0:CELLS, :] = v_ref[:, mine]
    keys[CELLS:, :] = dot(outside[...], wk_ref[:, mine]).astype(bf16)
    values[CELLS:, :] = dot(outside[...], wv_ref[:, mine]).astype(bf16)
    rest_ref[:, :SIDE] = dot(outside[...], wk_ref[:, rest]).astype(bf16)
    rest_ref[:, SIDE:] = dot(outside[...], wv_ref[:, rest]).astype(bf16)
    attend(near_ref, count_ref, side, q_ref, g_ref, out_ref, keys, values, keys_t, values_t, bias)


def attend_second_kernel(near_ref, count_ref, side_ref, q_ref, k_ref, v_ref, g_ref, rest_ref,
                         out_ref, keys, values, keys_t, values_t, bias):
    side = side_ref[0]
    mine = pl.ds(pl.multiple_of(side * SIDE, SIDE), SIDE)
    keys[0:CELLS, :] = k_ref[:, mine]
    values[0:CELLS, :] = v_ref[:, mine]
    keys[CELLS:, :] = rest_ref[:, :SIDE]
    values[CELLS:, :] = rest_ref[:, SIDE:]
    attend(near_ref, count_ref, side, q_ref, g_ref, out_ref, keys, values, keys_t, values_t, bias)


def attend(near_ref, count_ref, side, q_ref, g_ref, out_ref, keys, values, keys_t, values_t, bias):
    first = pl.multiple_of(side * SIDE, SIDE)
    keys_t[...] = keys[...].T
    values_t[...] = values[...].T

    row = lax.broadcasted_iota(jnp.int32, (BS, BS), 0)
    for block in range(4):
        for j in range(2):
            used = (near_ref[j, 0] == block) | (near_ref[j, 1] == block) | (near_ref[j, 2] == block)
            live = jnp.where(used, BS if block < 2 else count_ref[max(block - 2, 0)], 0)
            bias[block * BS:(block + 1) * BS, j * BS:(j + 1) * BS] = jnp.where(row < live, 0.0, MASKED)

    lane = lax.broadcasted_iota(jnp.int32, (CELLS, PAIR), 1)

    def softmax(scores):
        highest = jnp.max(scores, axis=0, keepdims=True)
        powers = jnp.exp(scores - highest)
        return powers * (1.0 / jnp.sum(powers, axis=0, keepdims=True))

    def score_grad(probs, prob_grad):
        weighted = probs * prob_grad
        return weighted - probs * jnp.sum(weighted, axis=0, keepdims=True)

    for pair in range(PAIRS):
        cols = slice(pair * PAIR, (pair + 1) * PAIR)
        k_pair = keys[:, cols]
        v_pair = values[:, cols]
        from_cols = pl.ds(pl.multiple_of(first + pair * PAIR, PAIR), PAIR)
        q_pair = q_ref[:, from_cols]
        g_pair = g_ref[:, from_cols]
        key_term = None
        value_term = None
        out_t = []
        qg_t = []
        for half in range(2):
            chosen = (lane >= HEAD) if half else (lane < HEAD)
            q_head = jnp.where(chosen, q_pair, jnp.zeros_like(q_pair))
            g_head = jnp.where(chosen, g_pair, jnp.zeros_like(g_pair))
            scores = dot(k_pair, q_head, NT)
            prob_grad = dot(v_pair, g_head, NT)
            near = softmax(scores[:POOL_ROWS] + bias[...])
            anchor = softmax(scores[POOL_ROWS:])
            probs = jnp.concatenate([near.astype(bf16), anchor.astype(bf16)], 0)
            grads = jnp.concatenate(
                [
                    score_grad(near, prob_grad[:POOL_ROWS]).astype(bf16),
                    score_grad(anchor, prob_grad[POOL_ROWS:]).astype(bf16),
                ],
                0,
            )
            head_rows = slice(pair * PAIR + half * HEAD, pair * PAIR + (half + 1) * HEAD)
            out_t.append(dot(values_t[head_rows, :], probs))
            qg_t.append(dot(keys_t[head_rows, :], grads) * SCALE)
            k_new = dot(grads, q_head)
            v_new = dot(probs, g_head)
            key_term = k_new if key_term is None else key_term + k_new
            value_term = v_new if value_term is None else value_term + v_new
        shifted_cols = slice(SIDE + pair * PAIR, SIDE + (pair + 1) * PAIR)
        out_ref[CELLS:CELLS + KEY_ROWS, cols] = key_term.astype(bf16)
        out_ref[CELLS:CELLS + KEY_ROWS, shifted_cols] = value_term.astype(bf16)
        out_ref[0:CELLS, cols] = jnp.concatenate(out_t, 0).astype(bf16).T
        out_ref[0:CELLS, shifted_cols] = jnp.concatenate(qg_t, 0).astype(bf16).T


def attend_scratch(extra):
    return [
        pltpu.VMEM((KEY_ROWS, SIDE), bf16),
        pltpu.VMEM((KEY_ROWS, SIDE), bf16),
        pltpu.VMEM((SIDE, KEY_ROWS), bf16),
        pltpu.VMEM((SIDE, KEY_ROWS), bf16),
        pltpu.VMEM((POOL_ROWS, CELLS), f32),
    ] + [pltpu.VMEM((POOL_ROWS, D), bf16)] * extra


def attend_first_call(near, count, side, queries, received, dy, wk, wv):
    smem = pl.BlockSpec(memory_space=pltpu.SMEM)
    vmem = pl.BlockSpec(memory_space=pltpu.VMEM)
    return pl.pallas_call(
        attend_first_kernel,
        in_specs=[smem] * 3 + [vmem] * 11,
        out_shape=[jax.ShapeDtypeStruct((2048, D), bf16), pltpu.HBM((POOL_ROWS, D), bf16)],
        scratch_shapes=attend_scratch(1),
        compiler_params=params(24),
    )(near, count, side, *queries[:4], *held(queries[4]), *received, *held(dy, wk, wv))


def attend_second_call(near, count, side, queries, rest):
    smem = pl.BlockSpec(memory_space=pltpu.SMEM)
    vmem = pl.BlockSpec(memory_space=pltpu.VMEM)
    return pl.pallas_call(
        attend_second_kernel,
        in_specs=[smem] * 3 + [vmem] * 5,
        out_shape=jax.ShapeDtypeStruct((1024, D), bf16),
        scratch_shapes=attend_scratch(0),
        compiler_params=params(24),
    )(near, count, side, *queries, *held(rest))


def outer_kernel(first_ref, own_ref, got_ref, parts):
    mine = slice(1024, 1024 + KEY_ROWS)

    def block(term, low, cols):
        starts = [48 * z + 24 * low for odd in range(2) for z in range(odd, 8, 2)]
        return jnp.concatenate([term[m:m + 24, cols] for m in starts], 0).astype(bf16)

    def put(slot, rows):
        parts[0, slot] = rows[:96]
        parts[1, slot] = rows[96:]

    def keep(matrix, term, cols):
        for high in range(2):
            for low in range(2):
                put(4 * matrix + 2 * high + low, block(term[high * SIDE:(high + 1) * SIDE], low, cols))

    left, right = slice(0, SIDE), slice(SIDE, D)
    keep(0, dot(first_ref[mine, :CELLS], own_ref[0:CELLS, right])
         + dot(got_ref[mine, :CELLS], got_ref[0:CELLS, right]), slice(None))
    pairs = (
        dot(first_ref[mine, :], own_ref[CELLS:1024, :])
        + dot(got_ref[mine, :], got_ref[CELLS:1024, :])
    )
    keep(1, pairs, left)
    keep(2, pairs, right)
    out_term = dot(own_ref[0:CELLS, left], first_ref[1024 + KEY_ROWS:, :], TN) + dot(
        got_ref[0:CELLS, left], got_ref[1024 + KEY_ROWS:, :], TN
    )
    for high in range(2):
        for low in range(2):
            put(12 + 2 * high + low, block(out_term, low, right if high else left))


def outer_call(first, own, got):
    return pl.pallas_call(
        outer_kernel,
        out_shape=pltpu.HBM((2, 16, 96, SIDE), bf16),
        compiler_params=params(32),
    )(first, own, got)


def plane_kernel(got_ref, out_ref):
    result = total([got_ref[index] for index in range(32)])
    for z in range(4):
        out_ref[z] = result[24 * z:24 * z + 24].astype(bf16)


def plane_call(got):
    return pl.pallas_call(
        plane_kernel,
        out_shape=jax.ShapeDtypeStruct((4, 24, SIDE), bf16),
        compiler_params=params(10),
    )(got)


def total(rows):
    result = rows[0].astype(f32)
    for row in rows[1:]:
        result = result + row.astype(f32)
    return result


def started(pairs, sems):
    copies = [pltpu.make_async_copy(src, dst, sems.at[i]) for i, (src, dst) in enumerate(pairs)]
    for copy in copies:
        copy.start()
    return copies


def waited(copies):
    for copy in copies:
        copy.wait()


def halves(core):
    return [pl.ds(pl.multiple_of(side * SIDE, SIDE), SIDE) for side in (core, 1 - core)]


def back_kernel(place_ref, x_ref, first_any, own_any, wq_any, wk_any, wv_any, wo_any, mixed_ref,
                ng_ref, lo_ref, hi_ref, a0_ref, a1_ref, a2_ref, a3_ref, rows, own_ref, first_ref,
                wq_ref, wk_ref, wv_ref, wo_ref, sems):
    loads = started(
        [
            (wk_any, wk_ref), (own_any, own_ref), (wv_any, wv_ref),
            (first_any.at[0:1024, :], first_ref), (wq_any, wq_ref), (wo_any, wo_ref),
        ],
        sems,
    )
    sources = list(zip((own_ref, first_ref), halves(place_ref[2])))
    waited(loads[:2])
    kv = dot(own_ref[CELLS:, :SIDE], wk_ref[:, sources[0][1]], NT)
    waited(loads[2:3])
    kv = kv + dot(own_ref[CELLS:, SIDE:], wv_ref[:, sources[0][1]], NT)
    waited(loads[3:])
    kv = kv + dot(first_ref[CELLS:, :SIDE], wk_ref[:, sources[1][1]], NT)
    kv = kv + dot(first_ref[CELLS:, SIDE:], wv_ref[:, sources[1][1]], NT)
    lo_ref[...] = kv[CELLS:CELLS + BS].astype(bf16)
    hi_ref[...] = kv[CELLS + BS:POOL_ROWS].astype(bf16)
    for y in range(4):
        rows[y] = kv[POOL_ROWS + 64 * y:POOL_ROWS + 64 * y + 64].astype(bf16)
    for step, target in enumerate((a0_ref, a1_ref, a2_ref, a3_ref)):
        target[...] = rows[(place_ref[1] + step) % 4]
    grad = kv[:CELLS]
    out = x_ref[...].astype(f32)
    for source, half in sources:
        grad = grad + dot(source[:CELLS, SIDE:], wq_ref[:, half], NT)
        out = out + dot(source[:CELLS, :SIDE], wo_ref[half, :])
    ng_ref[...] = grad
    mixed_ref[...] = out.astype(bf16)


def back_call(place, x, first, own, wq, wk, wv, wo):
    smem = pl.BlockSpec(memory_space=pltpu.SMEM)
    whole = pl.BlockSpec(memory_space=pltpu.VMEM)
    anywhere = pl.BlockSpec(memory_space=pl.ANY)
    return pl.pallas_call(
        back_kernel,
        in_specs=[smem, whole] + [anywhere] * 6,
        out_shape=[jax.ShapeDtypeStruct((CELLS, D), bf16), pltpu.HBM((CELLS, D), f32)]
        + [jax.ShapeDtypeStruct((BS, D), bf16)] * 2
        + [jax.ShapeDtypeStruct((64, D), bf16)] * 4,
        scratch_shapes=[pltpu.VMEM((4, 64, D), bf16)]
        + [pltpu.VMEM((1024, D), bf16)] * 2
        + [pltpu.VMEM((D, D), bf16)] * 4
        + [pltpu.SemaphoreType.DMA((6,))],
        compiler_params=params(24),
    )(place, *held(x, first, own, wq, wk, wv, wo))


def share_kernel(place_ref, s0, s1, s2, s3, keep_ref, send_ref, rows):
    summed = total([ref[...] for ref in (s0, s1, s2, s3)])
    rows[0] = summed[:32]
    rows[1] = summed[32:]
    xh = place_ref[0] // 2
    keep_ref[...] = rows[xh]
    send_ref[...] = rows[1 - xh].astype(bf16)


def share_call(place, shares):
    smem = pl.BlockSpec(memory_space=pltpu.SMEM)
    vmem = pl.BlockSpec(memory_space=pltpu.VMEM)
    return pl.pallas_call(
        share_kernel,
        in_specs=[smem] + [vmem] * 4,
        out_shape=[pltpu.HBM((32, D), f32), jax.ShapeDtypeStruct((32, D), bf16)],
        scratch_shapes=[pltpu.VMEM((2, 32, D), f32)],
        compiler_params=params(4),
    )(place, *shares)


def final_kernel(x_ref, dy_ref, own_ref, lo_ref, hi_ref, anchor_ref, face_ref, kept_ref, crossed_ref,
                 out_ref):
    x = x_ref[...].astype(f32)
    inverse = lax.rsqrt(jnp.mean(x * x, axis=-1, keepdims=True) + EPSILON)

    def placed(index_row, rows):
        cells = lax.broadcasted_iota(jnp.int32, (CELLS, index_row.shape[1]), 0)
        return dot((cells == index_row).astype(bf16), rows)

    shares = kept_ref[...] + crossed_ref[...].astype(f32)
    high = shares.astype(bf16)
    low = (shares - high.astype(f32)).astype(bf16)
    normed_grad = (
        own_ref[...]
        + placed(face_ref[0:1, :], lo_ref[...])
        + placed(face_ref[1:2, :], hi_ref[...])
        + placed(anchor_ref[...], high)
        + placed(anchor_ref[...], low)
    )
    cube = inverse * inverse * inverse
    out_ref[...] = (
        dy_ref[...].astype(f32)
        + inverse * normed_grad
        - x * cube * jnp.mean(normed_grad * x, axis=-1, keepdims=True)
    ).astype(bf16)


def final_call(x, dy, own, from_lo, from_hi, anchor_row, face_rows, kept, crossed):
    return pl.pallas_call(
        final_kernel,
        out_shape=jax.ShapeDtypeStruct((CELLS, D), bf16),
        compiler_params=params(12),
    )(*held(x, dy, own), from_lo, from_hi, *held(anchor_row, face_rows, kept), crossed)


def swapped(value, axis):
    return lax.ppermute(value, axis, [(0, 1), (1, 0)])


def spread(arrays, axis):
    return [arrays[0]] + [
        lax.ppermute(arrays[k], axis, [(i, (i + k) % 4) for i in range(4)]) for k in (1, 2, 3)
    ]


def along(value, step):
    count = 32
    pairs = [(i, i + step) for i in range(count) if 0 <= i + step < count]
    return lax.ppermute(value, ("zh", "zl", "xl", "core"), pairs)


X_RING = ("xh", "xl")
SLOT = ("y", "xh")


def settle_kernel(place_ref, rows_ref, own_ref, other_ref):
    rows = total([rows_ref[index] for index in range(4)])
    upper = jnp.where(place_ref[1] == 3, place_ref[0] // 2, place_ref[2]) == 1
    own_ref[...] = jnp.where(upper, rows[12:], rows[:12])
    other_ref[...] = jnp.where(upper, rows[:12], rows[12:])


def settle_call(place, rows):
    smem = pl.BlockSpec(memory_space=pltpu.SMEM)
    vmem = pl.BlockSpec(memory_space=pltpu.VMEM)
    return pl.pallas_call(
        settle_kernel,
        in_specs=[smem, vmem],
        out_shape=[jax.ShapeDtypeStruct((12, SIDE), f32)] * 2,
        compiler_params=params(4),
    )(place, rows)


def settled(place, rows):
    own, other = settle_call(place, rows)
    last = place[1] == 3
    core = place[2]

    def device(y_at, xh_at, core_at):
        return (y_at * 2 + xh_at) * 2 + core_at

    turn, swap = [], []
    for h in range(2):
        for r in range(2):
            turn.append((device(3, h, r), device(3, r, h)))
            swap.append((device(3, h, r), device(3, r, 1 - h)))
            swap += [(device(m, h, r), device(m, h, 1 - r)) for m in range(3)]
    axes = ("y", "xh", "core")
    turned = lax.ppermute(own, axes, turn)
    here = jnp.where(last, turned, own)
    there = lax.ppermute(other, axes, swap)
    return jnp.where(
        core == 0, jnp.concatenate([here, there], 1), jnp.concatenate([there, here], 1)
    )


def body(
    cell_features,
    cotangent,
    query_weight,
    key_weight,
    value_weight,
    out_weight,
    anchor_index,
    face_cells,
    halo_count,
    neighbour_blocks,
):
    x = cell_features[0]
    dy = cotangent[0]
    face_rows = face_cells.reshape(2, BS)
    near = neighbour_blocks.reshape(2, NB)
    count = halo_count.reshape(2)
    weights = (query_weight, key_weight, value_weight, out_weight)
    core = lax.axis_index("core").astype(jnp.int32).reshape(1)
    place = jnp.stack(
        [2 * lax.axis_index("xh") + lax.axis_index("xl"), lax.axis_index("y"), core[0]]
    ).astype(jnp.int32)

    normed, sent_anchors, sent_lo, sent_hi = send_call(x, anchor_index, face_rows)
    from_lo = along(sent_hi, 1)
    from_hi = along(sent_lo, -1)
    anchors = lax.all_to_all(sent_anchors, SLOT, 0, 0, tiled=True)
    q, k, v, g = project_call(normed, dy, *weights)

    first, rest = attend_first_call(
        near, count, 1 - core, (q, k, v, g, normed), (from_lo, from_hi, anchors), dy,
        key_weight, value_weight,
    )
    got = swapped(first, "core")
    own = attend_second_call(near, count, core, (q, k, v, g), rest)

    parts = outer_call(first, own, got)
    own, parts = lax.optimization_barrier((own, parts))
    plane = lax.all_to_all(parts.reshape(32, 96, SIDE), ("zl", "y", "xh", "xl"), 0, 0, tiled=True)
    mixed, own_grad, to_lo, to_hi, *shares = back_call(place, x, first, own, *weights)
    shares = spread(shares, "y")
    back_hi = along(to_lo, -1)
    back_lo = along(to_hi, 1)
    plane, back_hi = lax.optimization_barrier((plane, back_hi))
    kept, crossing = share_call(place, shares)
    crossed = swapped(crossing, "xh")
    column = plane_call(plane)
    column, back_hi, back_lo = lax.optimization_barrier((column, back_hi, back_lo))
    column = lax.all_to_all(column, "zh", 0, 0, tiled=True)
    column, own_grad = lax.optimization_barrier((column, own_grad))
    cell_grad = final_call(
        x, dy, own_grad, back_lo, back_hi, anchor_index, face_rows, kept, crossed
    )
    weight_grads = settled(place, column)
    return mixed[None], cell_grad[None], weight_grads


def solution(mesh):
    fine = Mesh(mesh.devices.reshape(4, 2, 4, 2, 2, 2), ("y", "xh", "zh", "zl", "xl", "core"))
    dom = ("zh", "zl", "xl", "core")
    blk = ("y", "xh")
    return jax.shard_map(
        body,
        mesh=fine,
        in_specs=(
            P(dom, blk, None),
            P(dom, blk, None),
            P(),
            P(),
            P(),
            P(),
            P(dom, blk),
            P(dom, blk, None, None),
            P(dom, blk, None),
            P(dom, blk, None),
        ),
        out_specs=(P(dom, blk, None), P(dom, blk, None), P(blk + dom, None)),
        check_vma=False,
    )
```

```python
import functools

import jax
import jax.numpy as jnp
from jax import lax
from jax.experimental import pallas as pl
from jax.experimental.pallas import tpu as pltpu
from jax.sharding import Mesh, PartitionSpec as P

HEADS = 12
BS = 128
NB = 3
D = 768
CELLS = 256
ANCHORS = 256
POOL_ROWS = 512
KEY_ROWS = 768
HEAD = 64
SIDE = 384
PAIRS = 3
SLOTS = 8
WIDE = (("zl", 2), ("xh", 2), ("y", 4), ("xl", 2))
PAIR = 128
SCALE = 0.125
EPSILON = 1e-06
MASKED = -1e30

f32 = jnp.float32
bf16 = jnp.bfloat16

NN = (((1,), (0,)), ((), ()))
NT = (((1,), (1,)), ((), ()))
TN = (((0,), (0,)), ((), ()))


def dot(a, b, dims=NN):
    return lax.dot_general(a, b, dims, preferred_element_type=f32)


def held(*arrays):
    return [pltpu.with_memory_space_constraint(a, pltpu.HBM) for a in arrays]


def params(mib):
    return pltpu.CompilerParams(vmem_limit_bytes=mib << 20)


def send_kernel(x_ref, anchor_ref, face_ref, normed_ref, rows_a_ref, rows_lo_ref, rows_hi_ref):
    x = x_ref[...].astype(f32)
    inverse = lax.rsqrt(jnp.mean(x * x, axis=-1, keepdims=True) + EPSILON)
    normed = (x * inverse).astype(bf16)
    normed_ref[...] = normed

    def picked(index_row):
        cells = lax.broadcasted_iota(jnp.int32, (CELLS, index_row.shape[1]), 0)
        one_hot = (cells == index_row).astype(bf16)
        return dot(one_hot, normed, TN).astype(bf16)

    anchor_rows = picked(anchor_ref[...])
    for slot in range(SLOTS):
        rows_a_ref[slot] = anchor_rows
    rows_lo_ref[...] = picked(face_ref[0:1, :])
    rows_hi_ref[...] = picked(face_ref[1:2, :])


def send_call(x, anchor_row, face_rows):
    return pl.pallas_call(
        send_kernel,
        out_shape=[
            pltpu.HBM((CELLS, D), bf16),
            pltpu.HBM((SLOTS, 32, D), bf16),
            jax.ShapeDtypeStruct((BS, D), bf16),
            jax.ShapeDtypeStruct((BS, D), bf16),
        ],
        compiler_params=params(8),
    )(*held(x, anchor_row, face_rows))


def project_kernel(n_ref, dy_ref, wq_ref, wk_ref, wv_ref, wo_ref, q_ref, k_ref, v_ref, g_ref):
    normed = n_ref[...]
    q_ref[...] = (dot(normed, wq_ref[...]).astype(bf16) * SCALE).astype(bf16)
    k_ref[...] = dot(normed, wk_ref[...]).astype(bf16)
    v_ref[...] = dot(normed, wv_ref[...]).astype(bf16)
    g_ref[...] = dot(dy_ref[...], wo_ref[...], NT).astype(bf16)


def project_call(normed, dy, wq, wk, wv, wo):
    return pl.pallas_call(
        project_kernel,
        out_shape=[jax.ShapeDtypeStruct((CELLS, D), bf16)] * 4,
        compiler_params=params(14),
    )(*held(normed, dy, wq, wk, wv, wo))


def attend_first_kernel(near_ref, count_ref, side_ref, q_ref, k_ref, v_ref, g_ref, n_ref, lo_ref,
                        hi_ref, an_ref, dy_ref, wk_ref, wv_ref, out_ref, rest_ref, keys, values,
                        keys_t, values_t, bias, outside):
    outside[0:BS, :] = lo_ref[...]
    outside[BS:2 * BS, :] = hi_ref[...]
    for slot in range(SLOTS):
        outside[2 * BS + 32 * slot:2 * BS + 32 * slot + 32, :] = an_ref[slot]
    out_ref[1024:1024 + KEY_ROWS, :CELLS] = n_ref[...].T
    out_ref[1024:1024 + KEY_ROWS, CELLS:] = outside[...].T
    out_ref[1024 + KEY_ROWS:, :] = dy_ref[...]
    side = side_ref[0]
    mine = pl.ds(pl.multiple_of(side * SIDE, SIDE), SIDE)
    rest = pl.ds(pl.multiple_of((1 - side) * SIDE, SIDE), SIDE)
    keys[0:CELLS, :] = k_ref[:, mine]
    values[0:CELLS, :] = v_ref[:, mine]
    keys[CELLS:, :] = dot(outside[...], wk_ref[:, mine]).astype(bf16)
    values[CELLS:, :] = dot(outside[...], wv_ref[:, mine]).astype(bf16)
    rest_ref[:, :SIDE] = dot(outside[...], wk_ref[:, rest]).astype(bf16)
    rest_ref[:, SIDE:] = dot(outside[...], wv_ref[:, rest]).astype(bf16)
    attend(near_ref, count_ref, side, q_ref, g_ref, out_ref, keys, values, keys_t, values_t, bias)


def attend_second_kernel(near_ref, count_ref, side_ref, q_ref, k_ref, v_ref, g_ref, rest_ref,
                         out_ref, keys, values, keys_t, values_t, bias):
    side = side_ref[0]
    mine = pl.ds(pl.multiple_of(side * SIDE, SIDE), SIDE)
    keys[0:CELLS, :] = k_ref[:, mine]
    values[0:CELLS, :] = v_ref[:, mine]
    keys[CELLS:, :] = rest_ref[:, :SIDE]
    values[CELLS:, :] = rest_ref[:, SIDE:]
    attend(near_ref, count_ref, side, q_ref, g_ref, out_ref, keys, values, keys_t, values_t, bias)


def attend(near_ref, count_ref, side, q_ref, g_ref, out_ref, keys, values, keys_t, values_t, bias):
    first = pl.multiple_of(side * SIDE, SIDE)
    keys_t[...] = keys[...].T
    values_t[...] = values[...].T

    row = lax.broadcasted_iota(jnp.int32, (BS, BS), 0)
    for block in range(4):
        for j in range(2):
            used = (near_ref[j, 0] == block) | (near_ref[j, 1] == block) | (near_ref[j, 2] == block)
            live = jnp.where(used, BS if block < 2 else count_ref[max(block - 2, 0)], 0)
            bias[block * BS:(block + 1) * BS, j * BS:(j + 1) * BS] = jnp.where(row < live, 0.0, MASKED)

    lane = lax.broadcasted_iota(jnp.int32, (CELLS, PAIR), 1)

    def softmax(scores):
        highest = jnp.max(scores, axis=0, keepdims=True)
        powers = jnp.exp(scores - highest)
        return powers * (1.0 / jnp.sum(powers, axis=0, keepdims=True))

    def score_grad(probs, prob_grad):
        weighted = probs * prob_grad
        return weighted - probs * jnp.sum(weighted, axis=0, keepdims=True)

    for pair in range(PAIRS):
        cols = slice(pair * PAIR, (pair + 1) * PAIR)
        k_pair = keys[:, cols]
        v_pair = values[:, cols]
        from_cols = pl.ds(pl.multiple_of(first + pair * PAIR, PAIR), PAIR)
        q_pair = q_ref[:, from_cols]
        g_pair = g_ref[:, from_cols]
        key_term = None
        value_term = None
        out_t = []
        qg_t = []
        for half in range(2):
            chosen = (lane >= HEAD) if half else (lane < HEAD)
            q_head = jnp.where(chosen, q_pair, jnp.zeros_like(q_pair))
            g_head = jnp.where(chosen, g_pair, jnp.zeros_like(g_pair))
            scores = dot(k_pair, q_head, NT)
            prob_grad = dot(v_pair, g_head, NT)
            near = softmax(scores[:POOL_ROWS] + bias[...])
            anchor = softmax(scores[POOL_ROWS:])
            probs = jnp.concatenate([near.astype(bf16), anchor.astype(bf16)], 0)
            grads = jnp.concatenate(
                [
                    score_grad(near, prob_grad[:POOL_ROWS]).astype(bf16),
                    score_grad(anchor, prob_grad[POOL_ROWS:]).astype(bf16),
                ],
                0,
            )
            head_rows = slice(pair * PAIR + half * HEAD, pair * PAIR + (half + 1) * HEAD)
            out_t.append(dot(values_t[head_rows, :], probs))
            qg_t.append(dot(keys_t[head_rows, :], grads) * SCALE)
            k_new = dot(grads, q_head)
            v_new = dot(probs, g_head)
            key_term = k_new if key_term is None else key_term + k_new
            value_term = v_new if value_term is None else value_term + v_new
        shifted_cols = slice(SIDE + pair * PAIR, SIDE + (pair + 1) * PAIR)
        out_ref[CELLS:CELLS + KEY_ROWS, cols] = key_term.astype(bf16)
        out_ref[CELLS:CELLS + KEY_ROWS, shifted_cols] = value_term.astype(bf16)
        out_ref[0:CELLS, cols] = jnp.concatenate(out_t, 0).astype(bf16).T
        out_ref[0:CELLS, shifted_cols] = jnp.concatenate(qg_t, 0).astype(bf16).T


def attend_scratch(extra):
    return [
        pltpu.VMEM((KEY_ROWS, SIDE), bf16),
        pltpu.VMEM((KEY_ROWS, SIDE), bf16),
        pltpu.VMEM((SIDE, KEY_ROWS), bf16),
        pltpu.VMEM((SIDE, KEY_ROWS), bf16),
        pltpu.VMEM((POOL_ROWS, CELLS), f32),
    ] + [pltpu.VMEM((POOL_ROWS, D), bf16)] * extra


def attend_first_call(near, count, side, queries, received, dy, wk, wv):
    smem = pl.BlockSpec(memory_space=pltpu.SMEM)
    vmem = pl.BlockSpec(memory_space=pltpu.VMEM)
    return pl.pallas_call(
        attend_first_kernel,
        in_specs=[smem] * 3 + [vmem] * 11,
        out_shape=[jax.ShapeDtypeStruct((2048, D), bf16), pltpu.HBM((POOL_ROWS, D), bf16)],
        scratch_shapes=attend_scratch(1),
        compiler_params=params(24),
    )(near, count, side, *queries[:4], *held(queries[4]), *received, *held(dy, wk, wv))


def attend_second_call(near, count, side, queries, rest):
    smem = pl.BlockSpec(memory_space=pltpu.SMEM)
    vmem = pl.BlockSpec(memory_space=pltpu.VMEM)
    return pl.pallas_call(
        attend_second_kernel,
        in_specs=[smem] * 3 + [vmem] * 5,
        out_shape=jax.ShapeDtypeStruct((1024, D), bf16),
        scratch_shapes=attend_scratch(0),
        compiler_params=params(24),
    )(near, count, side, *queries, *held(rest))


def outer_kernel(first_ref, own_ref, got_ref, parts):
    mine = slice(1024, 1024 + KEY_ROWS)

    def block(term, low, cols):
        starts = [48 * z + 24 * low for odd in range(2) for z in range(odd, 8, 2)]
        return jnp.concatenate([term[m:m + 24, cols] for m in starts], 0).astype(bf16)

    def put(matrix, high, low, rows):
        place = {"y": matrix, "xh": high, "xl": low}
        for odd in range(2):
            slot = 0
            for axis, size in WIDE:
                slot = slot * size + (odd if axis == "zl" else place[axis])
            parts[slot] = rows[96 * odd:96 * odd + 96]

    def keep(matrix, term, cols):
        for high in range(2):
            for low in range(2):
                put(matrix, high, low, block(term[high * SIDE:(high + 1) * SIDE], low, cols))

    left, right = slice(0, SIDE), slice(SIDE, D)
    keep(0, dot(first_ref[mine, :CELLS], own_ref[0:CELLS, right])
         + dot(got_ref[mine, :CELLS], got_ref[0:CELLS, right]), slice(None))
    pairs = (
        dot(first_ref[mine, :], own_ref[CELLS:1024, :])
        + dot(got_ref[mine, :], got_ref[CELLS:1024, :])
    )
    keep(1, pairs, left)
    keep(2, pairs, right)
    out_term = dot(own_ref[0:CELLS, left], first_ref[1024 + KEY_ROWS:, :], TN) + dot(
        got_ref[0:CELLS, left], got_ref[1024 + KEY_ROWS:, :], TN
    )
    for high in range(2):
        for low in range(2):
            put(3, high, low, block(out_term, low, right if high else left))


def outer_call(first, own, got):
    return pl.pallas_call(
        outer_kernel,
        out_shape=pltpu.HBM((32, 96, SIDE), bf16),
        compiler_params=params(32),
    )(first, own, got)


def plane_kernel(got_ref, out_ref):
    result = total([got_ref[index] for index in range(32)])
    for z in range(4):
        out_ref[z] = result[24 * z:24 * z + 24].astype(bf16)


def plane_call(got):
    return pl.pallas_call(
        plane_kernel,
        out_shape=jax.ShapeDtypeStruct((4, 24, SIDE), bf16),
        compiler_params=params(10),
    )(got)


def total(rows):
    result = rows[0].astype(f32)
    for row in rows[1:]:
        result = result + row.astype(f32)
    return result


def started(pairs, sems):
    copies = [pltpu.make_async_copy(src, dst, sems.at[i]) for i, (src, dst) in enumerate(pairs)]
    for copy in copies:
        copy.start()
    return copies


def waited(copies):
    for copy in copies:
        copy.wait()


def halves(core):
    return [pl.ds(pl.multiple_of(side * SIDE, SIDE), SIDE) for side in (core, 1 - core)]


def back_kernel(place_ref, x_ref, first_any, own_any, wq_any, wk_any, wv_any, wo_any, mixed_ref,
                ng_ref, lo_ref, hi_ref, a0_ref, a1_ref, a2_ref, a3_ref, rows, own_ref, first_ref,
                wq_ref, wk_ref, wv_ref, wo_ref, sems):
    loads = started(
        [
            (wk_any, wk_ref), (own_any, own_ref), (wv_any, wv_ref),
            (first_any.at[0:1024, :], first_ref), (wq_any, wq_ref), (wo_any, wo_ref),
        ],
        sems,
    )
    sources = list(zip((own_ref, first_ref), halves(place_ref[2])))
    waited(loads[:2])
    kv = dot(own_ref[CELLS:, :SIDE], wk_ref[:, sources[0][1]], NT)
    waited(loads[2:3])
    kv = kv + dot(own_ref[CELLS:, SIDE:], wv_ref[:, sources[0][1]], NT)
    waited(loads[3:])
    kv = kv + dot(first_ref[CELLS:, :SIDE], wk_ref[:, sources[1][1]], NT)
    kv = kv + dot(first_ref[CELLS:, SIDE:], wv_ref[:, sources[1][1]], NT)
    lo_ref[...] = kv[CELLS:CELLS + BS].astype(bf16)
    hi_ref[...] = kv[CELLS + BS:POOL_ROWS].astype(bf16)
    for y in range(4):
        rows[y] = kv[POOL_ROWS + 64 * y:POOL_ROWS + 64 * y + 64].astype(bf16)
    for step, target in enumerate((a0_ref, a1_ref, a2_ref, a3_ref)):
        target[...] = rows[(place_ref[1] + step) % 4]
    grad = kv[:CELLS]
    out = x_ref[...].astype(f32)
    for source, half in sources:
        grad = grad + dot(source[:CELLS, SIDE:], wq_ref[:, half], NT)
        out = out + dot(source[:CELLS, :SIDE], wo_ref[half, :])
    ng_ref[...] = grad
    mixed_ref[...] = out.astype(bf16)


def back_call(place, x, first, own, wq, wk, wv, wo):
    smem = pl.BlockSpec(memory_space=pltpu.SMEM)
    whole = pl.BlockSpec(memory_space=pltpu.VMEM)
    anywhere = pl.BlockSpec(memory_space=pl.ANY)
    return pl.pallas_call(
        back_kernel,
        in_specs=[smem, whole] + [anywhere] * 6,
        out_shape=[jax.ShapeDtypeStruct((CELLS, D), bf16), pltpu.HBM((CELLS, D), f32)]
        + [jax.ShapeDtypeStruct((BS, D), bf16)] * 2
        + [jax.ShapeDtypeStruct((64, D), bf16)] * 4,
        scratch_shapes=[pltpu.VMEM((4, 64, D), bf16)]
        + [pltpu.VMEM((1024, D), bf16)] * 2
        + [pltpu.VMEM((D, D), bf16)] * 4
        + [pltpu.SemaphoreType.DMA((6,))],
        compiler_params=params(24),
    )(place, *held(x, first, own, wq, wk, wv, wo))


def share_kernel(place_ref, s0, s1, s2, s3, keep_ref, send_ref, rows):
    summed = total([ref[...] for ref in (s0, s1, s2, s3)])
    rows[0] = summed[:32]
    rows[1] = summed[32:]
    xh = place_ref[0] // 2
    keep_ref[...] = rows[xh]
    send_ref[...] = rows[1 - xh].astype(bf16)


def share_call(place, shares):
    smem = pl.BlockSpec(memory_space=pltpu.SMEM)
    vmem = pl.BlockSpec(memory_space=pltpu.VMEM)
    return pl.pallas_call(
        share_kernel,
        in_specs=[smem] + [vmem] * 4,
        out_shape=[pltpu.HBM((32, D), f32), jax.ShapeDtypeStruct((32, D), bf16)],
        scratch_shapes=[pltpu.VMEM((2, 32, D), f32)],
        compiler_params=params(4),
    )(place, *shares)


def final_kernel(x_ref, dy_ref, own_ref, lo_ref, hi_ref, anchor_ref, face_ref, kept_ref, crossed_ref,
                 out_ref):
    x = x_ref[...].astype(f32)
    inverse = lax.rsqrt(jnp.mean(x * x, axis=-1, keepdims=True) + EPSILON)

    def placed(index_row, rows):
        cells = lax.broadcasted_iota(jnp.int32, (CELLS, index_row.shape[1]), 0)
        return dot((cells == index_row).astype(bf16), rows)

    shares = kept_ref[...] + crossed_ref[...].astype(f32)
    high = shares.astype(bf16)
    low = (shares - high.astype(f32)).astype(bf16)
    normed_grad = (
        own_ref[...]
        + placed(face_ref[0:1, :], lo_ref[...])
        + placed(face_ref[1:2, :], hi_ref[...])
        + placed(anchor_ref[...], high)
        + placed(anchor_ref[...], low)
    )
    cube = inverse * inverse * inverse
    out_ref[...] = (
        dy_ref[...].astype(f32)
        + inverse * normed_grad
        - x * cube * jnp.mean(normed_grad * x, axis=-1, keepdims=True)
    ).astype(bf16)


def final_call(x, dy, own, from_lo, from_hi, anchor_row, face_rows, kept, crossed):
    return pl.pallas_call(
        final_kernel,
        out_shape=jax.ShapeDtypeStruct((CELLS, D), bf16),
        compiler_params=params(12),
    )(*held(x, dy, own), from_lo, from_hi, *held(anchor_row, face_rows, kept), crossed)


def swapped(value, axis):
    return lax.ppermute(value, axis, [(0, 1), (1, 0)])


def spread(arrays, axis):
    return [arrays[0]] + [
        lax.ppermute(arrays[k], axis, [(i, (i + k) % 4) for i in range(4)]) for k in (1, 2, 3)
    ]


def along(value, step):
    count = 32
    pairs = [(i, i + step) for i in range(count) if 0 <= i + step < count]
    return lax.ppermute(value, ("zh", "zl", "xl", "core"), pairs)


X_RING = ("xh", "xl")
SLOT = ("y", "xh")


def settle_kernel(place_ref, rows_ref, own_ref, other_ref):
    rows = total([rows_ref[index] for index in range(4)])
    upper = jnp.where(place_ref[1] == 3, place_ref[0] // 2, place_ref[2]) == 1
    own_ref[...] = jnp.where(upper, rows[12:], rows[:12])
    other_ref[...] = jnp.where(upper, rows[:12], rows[12:])


def settle_call(place, rows):
    smem = pl.BlockSpec(memory_space=pltpu.SMEM)
    vmem = pl.BlockSpec(memory_space=pltpu.VMEM)
    return pl.pallas_call(
        settle_kernel,
        in_specs=[smem, vmem],
        out_shape=[jax.ShapeDtypeStruct((12, SIDE), f32)] * 2,
        compiler_params=params(4),
    )(place, rows)


def settled(place, rows):
    own, other = settle_call(place, rows)
    last = place[1] == 3
    core = place[2]

    def device(y_at, xh_at, core_at):
        return (y_at * 2 + xh_at) * 2 + core_at

    turn, swap = [], []
    for h in range(2):
        for r in range(2):
            turn.append((device(3, h, r), device(3, r, h)))
            swap.append((device(3, h, r), device(3, r, 1 - h)))
            swap += [(device(m, h, r), device(m, h, 1 - r)) for m in range(3)]
    axes = ("y", "xh", "core")
    turned = lax.ppermute(own, axes, turn)
    here = jnp.where(last, turned, own)
    there = lax.ppermute(other, axes, swap)
    return jnp.where(
        core == 0, jnp.concatenate([here, there], 1), jnp.concatenate([there, here], 1)
    )


def body(
    cell_features,
    cotangent,
    query_weight,
    key_weight,
    value_weight,
    out_weight,
    anchor_index,
    face_cells,
    halo_count,
    neighbour_blocks,
):
    x = cell_features[0]
    dy = cotangent[0]
    face_rows = face_cells.reshape(2, BS)
    near = neighbour_blocks.reshape(2, NB)
    count = halo_count.reshape(2)
    weights = (query_weight, key_weight, value_weight, out_weight)
    core = lax.axis_index("core").astype(jnp.int32).reshape(1)
    place = jnp.stack(
        [2 * lax.axis_index("xh") + lax.axis_index("xl"), lax.axis_index("y"), core[0]]
    ).astype(jnp.int32)

    normed, sent_anchors, sent_lo, sent_hi = send_call(x, anchor_index, face_rows)
    from_lo = along(sent_hi, 1)
    from_hi = along(sent_lo, -1)
    anchors = lax.all_to_all(sent_anchors, SLOT, 0, 0, tiled=True)
    q, k, v, g = project_call(normed, dy, *weights)

    first, rest = attend_first_call(
        near, count, 1 - core, (q, k, v, g, normed), (from_lo, from_hi, anchors), dy,
        key_weight, value_weight,
    )
    got = swapped(first, "core")
    own = attend_second_call(near, count, core, (q, k, v, g), rest)

    parts = outer_call(first, own, got)
    own, parts = lax.optimization_barrier((own, parts))
    plane = lax.all_to_all(parts, tuple(axis for axis, _ in WIDE), 0, 0, tiled=True)
    mixed, own_grad, to_lo, to_hi, *shares = back_call(place, x, first, own, *weights)
    shares = spread(shares, "y")
    back_hi = along(to_lo, -1)
    back_lo = along(to_hi, 1)
    plane, back_hi = lax.optimization_barrier((plane, back_hi))
    kept, crossing = share_call(place, shares)
    crossed = swapped(crossing, "xh")
    column = plane_call(plane)
    column, back_hi, back_lo = lax.optimization_barrier((column, back_hi, back_lo))
    column = lax.all_to_all(column, "zh", 0, 0, tiled=True)
    column, own_grad = lax.optimization_barrier((column, own_grad))
    cell_grad = final_call(
        x, dy, own_grad, back_lo, back_hi, anchor_index, face_rows, kept, crossed
    )
    weight_grads = settled(place, column)
    return mixed[None], cell_grad[None], weight_grads


def solution(mesh):
    fine = Mesh(mesh.devices.reshape(4, 2, 4, 2, 2, 2), ("y", "xh", "zh", "zl", "xl", "core"))
    dom = ("zh", "zl", "xl", "core")
    blk = ("y", "xh")
    return jax.shard_map(
        body,
        mesh=fine,
        in_specs=(
            P(dom, blk, None),
            P(dom, blk, None),
            P(),
            P(),
            P(),
            P(),
            P(dom, blk),
            P(dom, blk, None, None),
            P(dom, blk, None),
            P(dom, blk, None),
        ),
        out_specs=(P(dom, blk, None), P(dom, blk, None), P(blk + dom, None)),
        check_vma=False,
    )
```
